32 devices in a mesh: grp: 2 (over y), seq: 8 (over z, x), mdl: 2 (over core).
Axes of the slice: x: 2, y: 2, z: 4, core: 2. Of those that a mesh axis runs over, the one named last changes fastest.
Arguments:
- vis_tokens: bfloat16 [2048, 1152], P(('grp', 'seq'), 'mdl'), parts along dimension 0, may hold values from -6 to 6
- merge_target: int32 [2048], P(('grp', 'seq')), parts along dimension 0, may hold values from 0 to 126, as said below
- merged_counts: int32 [16], P('grp'), parts along dimension 0, may hold values from 43 to 127, as said below
- proj_weight: bfloat16 [1152, 3584], P('mdl'), may hold values from -0.1875 to 0.1875
- norm_gain: float32 [3584], replicated, may hold values from 0.1 to 1.9
- query_weight: bfloat16 [3584, 1792], P('seq', 'mdl'), may hold values from -0.09375 to 0.09375
- keyval_weight: bfloat16 [3584, 2, 256], P('seq', 'mdl'), may hold values from -0.09375 to 0.09375
- cache_kv: bfloat16 [512, 2, 256], P(('grp', 'seq'), 'mdl'), parts along dimension 0, may hold values from -40 to 40
Outputs:
- attn_out: bfloat16 [64, 16, 1792], P(None, ('grp', 'seq'), 'mdl'), parts along dimension 1
- new_kv: bfloat16 [64, 16, 2, 256], P(None, ('grp', 'seq'), 'mdl'), parts along dimension 1
The draws below stay inside these ranges and needn't reach their ends.
There are 2 independent parts, one for each index of `grp`. The reference program is written for one: setup_inputs(seed, part) draws one part's arguments, and reference() takes and returns one part's arrays. A program takes and returns all parts, laid end to end along the dimension named above; an argument that names none is the same for every part. Nothing has to cross between parts.
Inputs may be any that keep to these rules, and one draw needn't show every extreme that they name: `merge_target`: each shard's targets lie below that shard's entry of merged_counts, and every row index below that entry is named by at least one token of the shard. `merged_counts`: the counts sum to 512.
All inputs are finite; a program needn't handle non-finite values.
Results may differ from the reference program's by a relative error of at most 0.011.
Values may be sent and summed in bfloat16 or wider, within the bound.
A program may use at most 64 MiB of HBM per device.

```python
import math
import jax
import jax.numpy as jnp
from jax import lax

DV = 1152
D = 3584
HD = 128
HQ = 14
KVH = 2
NEW_DEV = 64
SHARDS = 8
TOK_IN = 128
SPIKE = 21
TOKENS = 1024
NEW_ROWS = 512
CACHE = 256


def shard_counts(key):
    order_key, depth_key = jax.random.split(key)
    device_order = jax.random.permutation(order_key, SHARDS)
    depths = jax.random.randint(depth_key, (SHARDS // 4,), 0, SPIKE + 1).at[0].set(SPIKE)
    role_ids = jnp.arange(SHARDS, dtype=jnp.int32) % 4
    depth_rows = jnp.repeat(depths, 4)
    values = jnp.where(role_ids == 0, NEW_DEV + 3 * depth_rows, NEW_DEV - depth_rows).astype(jnp.int32)
    return jnp.zeros((SHARDS,), jnp.int32).at[device_order].set(values)


def shard_order(shard_key):
    return jax.random.permutation(shard_key, TOK_IN)


def draw_merged_counts(key, part):
    counts = shard_counts(key)
    return counts


def draw_merge_target(key, part):
    counts = shard_counts(key)
    key = jax.random.fold_in(key, 7)
    order_key, extra_key = jax.random.split(key)
    shard_keys = jax.random.split(order_key, SHARDS)
    orders = jax.vmap(shard_order)(shard_keys)
    rank_ids = jnp.argsort(orders, axis=1, stable=True).astype(jnp.int32)
    spare_ids = jax.random.randint(extra_key, (SHARDS, TOK_IN), 0, 1 << 20)
    limits = counts[:, None]
    target = jnp.where(rank_ids < limits, rank_ids, spare_ids % limits)
    return target.reshape(-1).astype(jnp.int32)


def draw_cache_kv(key, part):
    key = jax.random.fold_in(key, 5)
    base_key = jax.random.fold_in(key, 0)
    array_shape = (CACHE, KVH, 2 * HD)
    whole = jnp.clip(jax.random.normal(base_key, array_shape, jnp.float32), -6.0, 6.0)
    return whole.astype(jnp.bfloat16)


def block_scale(own_key, extent, cuts, smallest, high):
    def one(axis_at, shards_of):
        heights = jax.random.uniform(jax.random.fold_in(jax.random.fold_in(own_key, 6), axis_at), (shards_of,), jnp.float32, smallest / len(cuts), high / len(cuts))
        return jnp.repeat(jnp.exp(heights), extent[axis_at] // shards_of).reshape((-1,) + (1,) * (len(extent) - axis_at - 1))

    factor_of = one(*cuts[0])
    for cut in cuts[1:]:
        factor_of = factor_of * one(*cut)
    return factor_of


def gaussian(key, dims, deviation, limit, cuts=(), kind=jnp.bfloat16):
    level = block_scale(key, dims, cuts, -0.22, 0.18) if cuts else 1.0
    array = jax.random.normal(key, dims, jnp.float32) * deviation * level
    return jnp.minimum(jnp.maximum(array, -limit), limit).astype(kind)


def setup_inputs(seed: int = 0, part: int = 0) -> dict:
    streams_of = jax.random.split(jax.random.key(seed), 9)
    own_keys = jax.random.split(jax.random.fold_in(streams_of[8], part), 9)
    vis_tokens = gaussian(own_keys[0], (TOKENS, DV), 1.0, 6.0, ((0, 8), (1, 2)))
    merge_target = draw_merge_target(jax.random.fold_in(jax.random.fold_in(streams_of[8], part), 71), part)
    merged_counts = draw_merged_counts(jax.random.fold_in(jax.random.fold_in(streams_of[8], part), 71), part)
    proj_weight = gaussian(streams_of[3], (DV, D), DV ** -0.5, 0.1875, ((0, 2),))
    norm_gain = jnp.clip(1.0 + 0.18 * jax.random.normal(streams_of[4], (D,), jnp.float32), 0.1, 1.9)
    query_weight = gaussian(streams_of[5], (D, HQ * HD), D ** -0.5, 0.09375, ((0, 8), (1, 2)))
    keyval_weight = gaussian(streams_of[6], (D, KVH, 2 * HD), D ** -0.5, 0.09375, ((0, 8), (1, 2)))
    cache_kv = draw_cache_kv(jax.random.fold_in(jax.random.fold_in(streams_of[8], part), 71), part)
    return dict(vis_tokens=vis_tokens, merge_target=merge_target, merged_counts=merged_counts, proj_weight=proj_weight, norm_gain=norm_gain, query_weight=query_weight, keyval_weight=keyval_weight, cache_kv=cache_kv)


theta_base = 1000000.0
norm_eps = 1e-06
mask_fill = -1e+30

def rotate(head_rows, positions):
    half_dim = head_rows.shape[-1] // 2
    frequency = jnp.power(theta_base, -2.0 * jnp.arange(half_dim, dtype=jnp.float32) / head_rows.shape[-1])
    angles = positions.astype(jnp.float32)[:, None] * frequency[None, :]
    cosine = jnp.concatenate([jnp.cos(angles), jnp.cos(angles)], axis=-1)[:, None, :]
    sine_part = jnp.concatenate([jnp.sin(angles), jnp.sin(angles)], axis=-1)[:, None, :]
    front_half = head_rows[..., :half_dim]
    back_half = head_rows[..., half_dim:]
    turned = jnp.concatenate([-back_half, front_half], axis=-1)
    return head_rows * cosine + turned * sine_part

def reference(vis_tokens, merge_target, merged_counts, proj_weight, norm_gain, query_weight, keyval_weight, cache_kv):
    offsets = (jnp.cumsum(merged_counts) - merged_counts).astype(jnp.int32)
    shard_of = jnp.arange(TOKENS, dtype=jnp.int32) // TOK_IN
    row_ids = (offsets[shard_of] + merge_target).astype(jnp.int32)
    summed = jax.ops.segment_sum(vis_tokens.astype(jnp.float32), row_ids, num_segments=NEW_ROWS)
    sizes = jax.ops.segment_sum(jnp.ones((TOKENS,), jnp.float32), row_ids, num_segments=NEW_ROWS)
    merged = (summed / sizes[:, None]).astype(jnp.bfloat16)
    pre_act = jnp.dot(merged, proj_weight, preferred_element_type=jnp.float32)
    activated = jax.nn.gelu(pre_act, approximate=False)
    inv_rms = lax.rsqrt(lax.optimization_barrier(jnp.mean(activated * activated, axis=1, keepdims=True)) + norm_eps)
    normed = (activated * inv_rms * norm_gain[None, :]).astype(jnp.bfloat16)
    positions = CACHE + jnp.arange(NEW_ROWS, dtype=jnp.int32)
    q_raw = jnp.dot(normed, query_weight, preferred_element_type=jnp.float32).reshape(NEW_ROWS, HQ, HD)
    queries = lax.optimization_barrier(rotate(q_raw, positions).astype(jnp.bfloat16))
    kv_raw = jnp.dot(normed, keyval_weight.reshape(D, KVH * 2 * HD), preferred_element_type=jnp.float32).reshape(NEW_ROWS, KVH, 2 * HD)
    fresh = jnp.concatenate([rotate(kv_raw[..., :HD], positions), kv_raw[..., HD:]], axis=-1).astype(jnp.bfloat16)
    context = lax.optimization_barrier(jnp.concatenate([cache_kv, fresh], axis=0))
    owner_head = jnp.arange(HQ, dtype=jnp.int32) // (HQ // KVH)
    key_rows = context[:, owner_head, :HD].astype(jnp.float32)
    value_rows = context[:, owner_head, HD:].astype(jnp.float32)
    key_index = jnp.arange(CACHE + NEW_ROWS, dtype=jnp.int32)
    block_rows = math.gcd(NEW_ROWS, 256)
    inv_scale = 1.0 / math.sqrt(HD)

    def attend(start):
        query_block = lax.dynamic_slice_in_dim(queries, start, block_rows, 0).astype(jnp.float32)
        query_pos = start + jnp.arange(block_rows, dtype=jnp.int32)
        visible = (key_index[None, :] < CACHE) | (key_index[None, :] - CACHE <= query_pos[:, None])
        scores = jnp.einsum('qhd,khd->hqk', query_block, key_rows) * inv_scale
        scores = jnp.where(visible[None], scores, mask_fill)
        row_max = lax.optimization_barrier(jnp.max(scores, axis=2, keepdims=True))
        weights = jnp.where(visible[None], jnp.exp(scores - row_max), 0.0)
        totals = lax.optimization_barrier(jnp.sum(weights, axis=2))
        rounded = lax.optimization_barrier(weights.astype(jnp.bfloat16)).astype(jnp.float32)
        mixed = jnp.einsum('hqk,khd->qhd', rounded, value_rows) / jnp.transpose(totals)[:, :, None]
        return mixed.astype(jnp.bfloat16)
    starts = jnp.arange(NEW_ROWS // block_rows, dtype=jnp.int32) * block_rows
    attended = lax.map(attend, starts).reshape(NEW_ROWS, HQ * HD)
    return (attended.reshape(NEW_DEV, SHARDS, HQ * HD), fresh.reshape(NEW_DEV, SHARDS, KVH, 2 * HD))
```

```python
import functools
import math

import jax
import jax.numpy as jnp
import numpy as np
from jax import lax
from jax.experimental import pallas as pl
from jax.experimental.pallas import tpu as pltpu
from jax.sharding import PartitionSpec as P

theta_base = 1000000.0
norm_eps = 1e-06
mask_fill = -1e30


def rotate(head_rows, positions):
    half_dim = head_rows.shape[-1] // 2
    frequency = jnp.power(
        theta_base, -2.0 * jnp.arange(half_dim, dtype=jnp.float32) / head_rows.shape[-1]
    )
    angles = positions.astype(jnp.float32)[:, None] * frequency[None, :]
    cosine = jnp.concatenate([jnp.cos(angles), jnp.cos(angles)], axis=-1)[:, None, :]
    sine_part = jnp.concatenate([jnp.sin(angles), jnp.sin(angles)], axis=-1)[:, None, :]
    front_half = head_rows[..., :half_dim]
    back_half = head_rows[..., half_dim:]
    turned = jnp.concatenate([-back_half, front_half], axis=-1)
    return head_rows * cosine + turned * sine_part


def plain_plan(
    vis_tokens,
    merge_target,
    merged_counts,
    proj_weight,
    norm_gain,
    query_weight,
    keyval_weight,
    cache_kv,
):
    shards = lax.axis_size("seq")
    device_index = lax.axis_index("seq")
    tok_in, width_in = vis_tokens.shape
    new_dev = tok_in // 2
    slot_cap = (new_dev + 3 * (new_dev // 3) + shards - 1) // shards
    offsets = jnp.cumsum(merged_counts) - merged_counts
    count_here = merged_counts[device_index]
    offset_here = offsets[device_index]
    slot_rows = jnp.arange(tok_in, dtype=jnp.int32)
    chosen = slot_rows[:, None] == merge_target[None, :]
    sizes = jnp.sum(chosen.astype(jnp.float32), axis=1)
    summed = jnp.dot(chosen.astype(jnp.bfloat16), vis_tokens, preferred_element_type=jnp.float32)
    merged = (summed / jnp.where(sizes > 0.0, sizes, 1.0)[:, None]).astype(jnp.bfloat16)
    peer_ids = jnp.arange(shards, dtype=jnp.int32)
    slot_ids = jnp.arange(slot_cap, dtype=jnp.int32)
    local_row = jnp.mod(peer_ids - offset_here, shards)[:, None] + slot_ids[None, :] * shards
    is_valid = local_row < count_here
    picked = jnp.take(merged, jnp.minimum(local_row, tok_in - 1).reshape(-1), axis=0).reshape(
        shards, slot_cap, width_in
    )
    outgoing = jnp.where(is_valid[:, :, None], picked, jnp.zeros_like(picked))
    incoming = lax.all_to_all(outgoing, "seq", split_axis=0, concat_axis=0, tiled=True)
    first_row = offsets + jnp.mod(device_index - offsets, shards)
    global_row = first_row[:, None] + slot_ids[None, :] * shards
    arrived = global_row < (offsets + merged_counts)[:, None]
    target = jnp.where(arrived, global_row // shards, -1).reshape(-1)
    placing = jnp.arange(new_dev, dtype=jnp.int32)[:, None] == target[None, :]
    arrived_rows = jnp.dot(
        placing.astype(jnp.bfloat16),
        incoming.reshape(shards * slot_cap, width_in),
        preferred_element_type=jnp.float32,
    ).astype(jnp.bfloat16)
    partial_pre = jnp.dot(arrived_rows, proj_weight, preferred_element_type=jnp.float32)
    pre_act = lax.psum(partial_pre, "mdl")
    activated = jax.nn.gelu(pre_act, approximate=False)
    inv_rms = lax.rsqrt(jnp.mean(activated * activated, axis=1, keepdims=True) + norm_eps)
    normed = (activated * inv_rms * norm_gain[None, :]).astype(jnp.bfloat16)

    def add_rows(piece):
        return jnp.dot(
            normed, piece.reshape(piece.shape[0], -1), preferred_element_type=jnp.float32
        )

    kv_heads = keyval_weight.shape[1]
    head_dim = keyval_weight.shape[2] // 2
    q_raw = add_rows(lax.all_gather(query_weight, "seq", axis=0, tiled=True))
    kv_raw = add_rows(lax.all_gather(keyval_weight, "seq", axis=0, tiled=True))
    cache_rows = cache_kv.shape[0]
    query_global = jnp.arange(new_dev, dtype=jnp.int32) * shards + device_index
    positions = cache_rows * shards + query_global
    heads_here = query_weight.shape[1] // head_dim
    group = heads_here // kv_heads
    queries = rotate(q_raw.reshape(new_dev, heads_here, head_dim), positions).astype(jnp.bfloat16)
    kv_rows = kv_raw.reshape(new_dev, kv_heads, 2 * head_dim)
    fresh = jnp.concatenate(
        [rotate(kv_rows[..., :head_dim], positions), kv_rows[..., head_dim:]], axis=-1
    ).astype(jnp.bfloat16)
    query_rows = (
        queries.reshape(new_dev, kv_heads, group, head_dim)
        .transpose(1, 0, 2, 3)
        .reshape(kv_heads, new_dev * group, head_dim)
    )
    query_pos = jnp.repeat(query_global, group)
    context = jnp.concatenate([cache_kv, fresh], axis=0)
    stride = cache_rows + new_dev
    inv_scale = 1.0 / math.sqrt(head_dim)

    def absorb(carried, key_block, visible):
        row_max, totals, accumulated = carried
        scores = (
            jnp.einsum(
                "hqd,khd->hqk",
                query_rows,
                key_block[:, :, :head_dim],
                preferred_element_type=jnp.float32,
            )
            * inv_scale
        )
        scores = jnp.where(visible[None], scores, mask_fill)
        new_max = jnp.maximum(row_max, jnp.max(scores, axis=2))
        weights = jnp.where(visible[None], jnp.exp(scores - new_max[:, :, None]), 0.0)
        factor = jnp.exp(row_max - new_max)
        totals = totals * factor + jnp.sum(weights, axis=2)
        mixed = jnp.einsum(
            "hqk,khd->hqd",
            weights.astype(jnp.bfloat16),
            key_block[:, :, head_dim:],
            preferred_element_type=jnp.float32,
        )
        accumulated = accumulated * factor[:, :, None] + mixed
        return (new_max, totals, accumulated)

    lanes = new_dev * group
    start_state = (
        jnp.full((kv_heads, lanes), mask_fill, jnp.float32),
        jnp.zeros((kv_heads, lanes), jnp.float32),
        jnp.zeros((kv_heads, lanes, head_dim), jnp.float32),
    )
    piece = lax.all_gather(context, "seq", axis=0, tiled=True)
    rows_in = piece.shape[0]
    padded_len = -(-rows_in // 128) * 128
    padded = piece
    tiles = padded_len // 128
    block_tiles = max((divisor for divisor in range(1, min(tiles, 8) + 1) if tiles % divisor == 0))
    block_len = 128 * block_tiles

    def fold_block(block_no, state_now):
        key_block = lax.dynamic_slice_in_dim(padded, block_no * block_len, block_len, 0)
        key_offset = block_no * block_len + jnp.arange(block_len, dtype=jnp.int32)
        source = key_offset // stride
        local_key = key_offset % stride
        key_global = (local_key - cache_rows) * shards + source
        present = (key_offset < rows_in)[None, :]
        visible = present & (
            (local_key < cache_rows)[None, :] | (key_global[None, :] <= query_pos[:, None])
        )
        return absorb(state_now, key_block, visible)

    row_max, totals, accumulated = lax.fori_loop(
        0, padded_len // block_len, fold_block, start_state
    )
    attended = (
        (accumulated / totals[:, :, None])
        .reshape(kv_heads, new_dev, group, head_dim)
        .transpose(1, 0, 2, 3)
    )
    attended = attended.reshape(new_dev, 1, heads_here * head_dim).astype(jnp.bfloat16)
    return (attended, fresh.reshape(new_dev, 1, kv_heads, 2 * head_dim))


MESH = pl.DeviceIdType.MESH
XS = 2


def fused_kernel(
    n,
    vis_ref,
    target_ref,
    counts_ref,
    gain_ref,
    proj_hbm,
    wq_hbm,
    wkv_hbm,
    cache_hbm,
    cos_hbm,
    sin_hbm,
    attn_ref,
    newkv_ref,
    proj,
    wq,
    wkv,
    cos_t,
    sin_t,
    cache_all,
    packed,
    incoming,
    pre,
    pre_recv,
    act,
    norm_send,
    norm_all,
    part_kv,
    part_q,
    xsend_kv,
    xrecv_kv,
    zsend_kv,
    zrecv_kv,
    xsend_q,
    xrecv_q,
    zsend_q,
    zrecv_q,
    fresh_all,
    q_rows,
    load_sem,
    s_cache,
    r_cache,
    s_tok,
    r_tok,
    s_pre,
    r_pre,
    s_norm,
    r_norm,
    s_fwd,
    r_fwd,
    s_x,
    r_x,
    s_z,
    r_z,
    s_fresh,
    r_fresh,
):
    s = lax.axis_index("seq")
    m = lax.axis_index("mdl")
    zs = n // XS
    z, x = s // XS, s % XS
    mate = {"mdl": 1 - m}
    peers = [(s + k) % n for k in range(n)]

    def send(src, dst, ssem, rsem, device):
        copy = pltpu.make_async_remote_copy(
            src_ref=src,
            dst_ref=dst,
            send_sem=ssem,
            recv_sem=rsem,
            device_id=device,
            device_id_type=MESH,
        )
        copy.start()
        return copy

    barrier = pltpu.get_barrier_semaphore()
    for k in range(1, n):
        pl.semaphore_signal(barrier, inc=1, device_id={"seq": peers[k]}, device_id_type=MESH)
    pl.semaphore_signal(barrier, inc=1, device_id=mate, device_id_type=MESH)

    loads = []
    for at, (src, dst) in enumerate(
        (
            (cache_hbm, cache_all.at[s]),
            (proj_hbm, proj),
            (wkv_hbm, wkv),
            (wq_hbm, wq),
            (cos_hbm.at[s], cos_t),
            (sin_hbm.at[s], sin_t),
        )
    ):
        copy = pltpu.make_async_copy(src, dst, load_sem.at[at])
        copy.start()
        loads.append(copy)

    toks = vis_ref.shape[0]
    cap = packed.shape[1]
    slots = n * cap
    new_dev = toks // 2
    prefix = []
    running = jnp.int32(0)
    here = jnp.int32(0)
    for i in range(n):
        prefix.append(running)
        here = jnp.where(s == i, running, here)
        running = running + counts_ref[i]
    slot = lax.broadcasted_iota(jnp.int32, (slots, toks), 0)
    local_row = ((slot // cap - here) & (n - 1)) + (slot % cap) * n
    chosen = jnp.where(local_row == target_ref[...], 1.0, 0.0)
    sizes = jnp.sum(chosen, axis=1, keepdims=True)
    summed = jnp.dot(
        chosen.astype(jnp.bfloat16), vis_ref[...], preferred_element_type=jnp.float32
    )
    merged = (summed / jnp.where(sizes > 0.0, sizes, 1.0)).astype(jnp.bfloat16)
    packed[...] = merged.reshape(packed.shape)

    pl.semaphore_wait(barrier, n)
    tok_copies = [
        send(packed.at[peers[k]], incoming.at[s], s_tok.at[k], r_tok.at[k], {"seq": peers[k]})
        for k in range(1, n)
    ]
    loads[0].wait()
    cache_copies = [
        send(cache_all.at[s], cache_all.at[s], s_cache.at[k], r_cache.at[k], {"seq": peers[k]})
        for k in range(1, n)
    ]
    incoming[s] = packed[s]

    column = lax.broadcasted_iota(jnp.int32, (new_dev, slots), 1)
    source = column // cap
    starts = jnp.zeros_like(column)
    ends = jnp.zeros_like(column)
    for i in range(n):
        starts = jnp.where(source == i, prefix[i], starts)
        ends = jnp.where(source == i, prefix[i] + counts_ref[i], ends)
    global_row = starts + ((s - starts) & (n - 1)) + (column % cap) * n
    goal = jnp.where(global_row < ends, global_row // n, -1)
    placing = jnp.where(
        goal == lax.broadcasted_iota(jnp.int32, (new_dev, slots), 0), 1.0, 0.0
    ).astype(jnp.bfloat16)
    loads[1].wait()
    for copy in tok_copies:
        copy.wait()
    rows = jnp.dot(
        placing,
        incoming[...].reshape(slots, incoming.shape[2]),
        preferred_element_type=jnp.float32,
    ).astype(jnp.bfloat16)

    width = proj.shape[1]
    half = new_dev // 2
    step = 512
    mine = pl.ds(pl.multiple_of(m * half, half), half)
    other = pl.ds(pl.multiple_of((1 - m) * half, half), half)
    pre_copies = []
    for c in range(width // step):
        cols = pl.ds(c * step, step)
        pre[c] = jnp.dot(rows, proj[:, cols], preferred_element_type=jnp.float32)
        pre_copies.append(
            send(pre.at[c, other], pre_recv.at[c], s_pre.at[c], r_pre.at[c], mate)
        )
    square = jnp.zeros((half, step), jnp.float32)
    for c in range(width // step):
        pre_copies[c].wait()
        value = pre[c, mine] + pre_recv[c]
        value = 0.5 * value * (1.0 + lax.erf(value * (1.0 / math.sqrt(2.0))))
        square = square + value * value
        act[:, pl.ds(c * step, step)] = value
    mean = jnp.sum(square, axis=1, keepdims=True) / width
    inv_rms = lax.rsqrt(mean + norm_eps)
    normed = (act[...] * inv_rms * gain_ref[...]).astype(jnp.bfloat16)
    depth = width // n
    for d in range(n):
        norm_send[d] = normed[:, d * depth : (d + 1) * depth]
    norm_copies = [
        send(norm_send.at[peers[k]], norm_all.at[s, m], s_norm.at[k], r_norm.at[k], {"seq": peers[k]})
        for k in range(1, n)
    ]
    norm_all[s, m] = norm_send[s]
    forwards = [send(norm_all.at[s, m], norm_all.at[s, m], s_fwd.at[0], r_fwd.at[0], mate)]
    for k in range(1, n):
        norm_copies[k - 1].wait()
        came = norm_all.at[(s + n - k) % n, m]
        forwards.append(send(came, came, s_fwd.at[k], r_fwd.at[k], mate))
    loads[2].wait()
    loads[3].wait()
    for copy in forwards:
        copy.wait()

    lhs = norm_all[...].reshape(n * new_dev, depth)
    x_copies = {}
    order = [(z + k) % zs for k in range(1, zs)] + [z]
    for which, weight, part, xsend, xrecv in (
        (0, wkv, part_kv, xsend_kv, xrecv_kv),
        (1, wq, part_q, xsend_q, xrecv_q),
    ):
        part[...] = jnp.dot(lhs, weight[...], preferred_element_type=jnp.float32).reshape(
            part.shape
        )
        for k, zt in enumerate(order):
            xsend[k] = part[zt * XS + 1 - x].astype(jnp.bfloat16)
            x_copies[which, k] = send(
                xsend.at[k],
                xrecv.at[k],
                s_x.at[which, k],
                r_x.at[which, k],
                {"seq": z * XS + 1 - x},
            )

    def along_z(which, part, xrecv, zsend, zrecv):
        copies = []
        for k in range(1, zs):
            zt = order[k - 1]
            x_copies[which, k - 1].wait()
            zsend[k - 1] = (
                part[zt * XS + x] + xrecv[k - 1].astype(jnp.float32)
            ).astype(jnp.bfloat16)
            copies.append(
                send(
                    zsend.at[k - 1],
                    zrecv.at[k - 1],
                    s_z.at[which, k - 1],
                    r_z.at[which, k - 1],
                    {"seq": zt * XS + x},
                )
            )
        x_copies[which, zs - 1].wait()
        return part[s] + xrecv[zs - 1].astype(jnp.float32), copies

    def finish(total, copies, zrecv):
        for k, copy in enumerate(copies):
            copy.wait()
            total = total + zrecv[k].astype(jnp.float32)
        return total

    head = cos_t.shape[1]
    loads[4].wait()
    loads[5].wait()
    cosine, sine = cos_t[...], sin_t[...]

    def turn(value):
        return value * cosine + pltpu.roll(value, head // 2, 1) * sine

    total, copies = along_z(0, part_kv, xrecv_kv, zsend_kv, zrecv_kv)
    total = finish(total, copies, zrecv_kv)
    fresh = jnp.concatenate([turn(total[:, :head]), total[:, head:]], axis=1).astype(jnp.bfloat16)
    fresh_all[s] = fresh
    newkv_ref[...] = fresh
    fresh_copies = [
        send(fresh_all.at[s], fresh_all.at[s], s_fresh.at[k], r_fresh.at[k], {"seq": peers[k]})
        for k in range(1, n)
    ]
    total, copies = along_z(1, part_q, xrecv_q, zsend_q, zrecv_q)
    total = finish(total, copies, zrecv_q)
    heads = total.shape[1] // head
    for h in range(heads):
        q_rows[pl.ds(h * new_dev, new_dev), :] = turn(
            total[:, h * head : (h + 1) * head]
        ).astype(jnp.bfloat16)
    for copy in cache_copies:
        copy.wait()
    for copy in fresh_copies:
        copy.wait()

    kept = cache_all.shape[0] * cache_all.shape[1]
    old = cache_all[...].reshape(kept, 2 * head)
    new = fresh_all[...].reshape(n * new_dev, 2 * head)
    queries = q_rows[...]
    contract = (((1,), (1,)), ((), ()))
    scale = 1.0 / math.sqrt(head)
    old_score = (
        lax.dot_general(queries, old[:, :head], contract, preferred_element_type=jnp.float32) * scale
    )
    new_score = (
        lax.dot_general(queries, new[:, :head], contract, preferred_element_type=jnp.float32) * scale
    )
    lanes = heads * new_dev
    key_at = lax.broadcasted_iota(jnp.int32, (lanes, n * new_dev), 1)
    query_at = lax.broadcasted_iota(jnp.int32, (lanes, n * new_dev), 0)
    visible = (key_at % new_dev) * n + key_at // new_dev <= (query_at % new_dev) * n + s
    new_score = jnp.where(visible, new_score, mask_fill)
    top = jnp.maximum(
        jnp.max(old_score, axis=1, keepdims=True), jnp.max(new_score, axis=1, keepdims=True)
    )
    old_weight = jnp.exp(old_score - top)
    new_weight = jnp.where(visible, jnp.exp(new_score - top), 0.0)
    totals = jnp.sum(old_weight, axis=1, keepdims=True) + jnp.sum(new_weight, axis=1, keepdims=True)
    mixed = jnp.dot(
        old_weight.astype(jnp.bfloat16), old[:, head:], preferred_element_type=jnp.float32
    ) + jnp.dot(new_weight.astype(jnp.bfloat16), new[:, head:], preferred_element_type=jnp.float32)
    attended = (mixed / totals).astype(jnp.bfloat16)
    for h in range(heads):
        attn_ref[:, pl.ds(h * head, head)] = attended[h * new_dev : (h + 1) * new_dev]


def fused_plan(
    vis_tokens,
    merge_target,
    merged_counts,
    proj_weight,
    norm_gain,
    query_weight,
    keyval_weight,
    cache_kv,
):
    n = lax.axis_size("seq")
    zs = n // XS
    toks, feat = vis_tokens.shape
    new_dev = toks // 2
    half = new_dev // 2
    cap = (new_dev + 3 * (new_dev // 3) + n - 1) // n
    width = proj_weight.shape[1]
    depth, qcols = query_weight.shape
    kvcols = keyval_weight.shape[2]
    head = kvcols // 2
    cached = cache_kv.shape[0]
    pos = (
        cached * n + np.arange(new_dev, dtype=np.float32)[None, :] * n
        + np.arange(n, dtype=np.float32)[:, None]
    ).astype(np.float32)
    freq = np.power(
        np.float32(theta_base), np.float32(-2.0) * np.arange(head // 2, dtype=np.float32) / np.float32(head)
    ).astype(np.float32)
    angles = (pos[:, :, None] * freq[None, None, :]).astype(np.float64)
    cos_table = np.concatenate([np.cos(angles)] * 2, axis=-1).astype(np.float32)
    sin_table = np.concatenate([-np.sin(angles), np.sin(angles)], axis=-1).astype(np.float32)
    bf, f32 = jnp.bfloat16, jnp.float32
    chunks = width // 512
    vm, dma = pltpu.VMEM, pltpu.SemaphoreType.DMA
    scratch = [
        vm((feat, width), bf),
        vm((depth, qcols), bf),
        vm((depth, kvcols), bf),
        vm((new_dev, head), f32),
        vm((new_dev, head), f32),
        vm((n, cached, kvcols), bf),
        vm((n, cap, feat), bf),
        vm((n, cap, feat), bf),
        vm((chunks, new_dev, 512), f32),
        vm((chunks, half, 512), f32),
        vm((half, width), f32),
        vm((n, half, depth), bf),
        vm((n, 2, half, depth), bf),
        vm((n, new_dev, kvcols), f32),
        vm((n, new_dev, qcols), f32),
        vm((zs, new_dev, kvcols), bf),
        vm((zs, new_dev, kvcols), bf),
        vm((zs - 1, new_dev, kvcols), bf),
        vm((zs - 1, new_dev, kvcols), bf),
        vm((zs, new_dev, qcols), bf),
        vm((zs, new_dev, qcols), bf),
        vm((zs - 1, new_dev, qcols), bf),
        vm((zs - 1, new_dev, qcols), bf),
        vm((n, new_dev, kvcols), bf),
        vm((qcols // head * new_dev, head), bf),
        dma((6,)),
        dma((n,)),
        dma((n,)),
        dma((n,)),
        dma((n,)),
        dma((chunks,)),
        dma((chunks,)),
        dma((n,)),
        dma((n,)),
        dma((n,)),
        dma((n,)),
        dma((2, zs)),
        dma((2, zs)),
        dma((2, zs)),
        dma((2, zs)),
        dma((n,)),
        dma((n,)),
    ]
    in_vmem = pl.BlockSpec(memory_space=pltpu.VMEM)
    anywhere = pl.BlockSpec(memory_space=pl.ANY)
    attended, fresh = pl.pallas_call(
        functools.partial(fused_kernel, n),
        out_shape=(
            jax.ShapeDtypeStruct((new_dev, qcols), bf),
            jax.ShapeDtypeStruct((new_dev, kvcols), bf),
        ),
        in_specs=[
            in_vmem,
            in_vmem,
            pl.BlockSpec(memory_space=pltpu.SMEM),
            in_vmem,
        ]
        + [anywhere] * 6,
        out_specs=(in_vmem, in_vmem),
        scratch_shapes=scratch,
        compiler_params=pltpu.CompilerParams(
            collective_id=0, has_side_effects=True, vmem_limit_bytes=48 * 1024 * 1024
        ),
    )(
        vis_tokens,
        merge_target.reshape(1, toks),
        merged_counts,
        norm_gain.reshape(1, width),
        proj_weight,
        query_weight,
        keyval_weight.reshape(depth, kvcols),
        cache_kv.reshape(cached, kvcols),
        jnp.asarray(cos_table),
        jnp.asarray(sin_table),
    )
    return (
        attended.reshape(new_dev, 1, qcols),
        fresh.reshape(new_dev, 1, keyval_weight.shape[1], kvcols),
    )


def solution(mesh):
    placed = (
        P(("grp", "seq"), "mdl"),
        P(("grp", "seq")),
        P("grp"),
        P("mdl", None),
        P(),
        P("seq", "mdl"),
        P("seq", "mdl", None),
        P(("grp", "seq"), "mdl", None),
    )
    per_device = fused_plan if mesh.shape["seq"] == 8 else plain_plan
    return jax.shard_map(
        per_device,
        mesh=mesh,
        in_specs=placed,
        out_specs=(P(None, ("grp", "seq"), "mdl"), P(None, ("grp", "seq"), "mdl", None)),
        check_vma=False,
    )
```

```python
import functools
import math

import jax
import jax.numpy as jnp
import numpy as np
from jax import lax
from jax.experimental import pallas as pl
from jax.experimental.pallas import tpu as pltpu
from jax.sharding import PartitionSpec as P

theta_base = 1000000.0
norm_eps = 1e-06
mask_fill = -1e30


def rotate(head_rows, positions):
    half_dim = head_rows.shape[-1] // 2
    frequency = jnp.power(
        theta_base, -2.0 * jnp.arange(half_dim, dtype=jnp.float32) / head_rows.shape[-1]
    )
    angles = positions.astype(jnp.float32)[:, None] * frequency[None, :]
    cosine = jnp.concatenate([jnp.cos(angles), jnp.cos(angles)], axis=-1)[:, None, :]
    sine_part = jnp.concatenate([jnp.sin(angles), jnp.sin(angles)], axis=-1)[:, None, :]
    front_half = head_rows[..., :half_dim]
    back_half = head_rows[..., half_dim:]
    turned = jnp.concatenate([-back_half, front_half], axis=-1)
    return head_rows * cosine + turned * sine_part


def plain_plan(
    vis_tokens,
    merge_target,
    merged_counts,
    proj_weight,
    norm_gain,
    query_weight,
    keyval_weight,
    cache_kv,
):
    shards = lax.axis_size("seq")
    device_index = lax.axis_index("seq")
    tok_in, width_in = vis_tokens.shape
    new_dev = tok_in // 2
    slot_cap = (new_dev + 3 * (new_dev // 3) + shards - 1) // shards
    offsets = jnp.cumsum(merged_counts) - merged_counts
    count_here = merged_counts[device_index]
    offset_here = offsets[device_index]
    slot_rows = jnp.arange(tok_in, dtype=jnp.int32)
    chosen = slot_rows[:, None] == merge_target[None, :]
    sizes = jnp.sum(chosen.astype(jnp.float32), axis=1)
    summed = jnp.dot(chosen.astype(jnp.bfloat16), vis_tokens, preferred_element_type=jnp.float32)
    merged = (summed / jnp.where(sizes > 0.0, sizes, 1.0)[:, None]).astype(jnp.bfloat16)
    peer_ids = jnp.arange(shards, dtype=jnp.int32)
    slot_ids = jnp.arange(slot_cap, dtype=jnp.int32)
    local_row = jnp.mod(peer_ids - offset_here, shards)[:, None] + slot_ids[None, :] * shards
    is_valid = local_row < count_here
    picked = jnp.take(merged, jnp.minimum(local_row, tok_in - 1).reshape(-1), axis=0).reshape(
        shards, slot_cap, width_in
    )
    outgoing = jnp.where(is_valid[:, :, None], picked, jnp.zeros_like(picked))
    incoming = lax.all_to_all(outgoing, "seq", split_axis=0, concat_axis=0, tiled=True)
    first_row = offsets + jnp.mod(device_index - offsets, shards)
    global_row = first_row[:, None] + slot_ids[None, :] * shards
    arrived = global_row < (offsets + merged_counts)[:, None]
    target = jnp.where(arrived, global_row // shards, -1).reshape(-1)
    placing = jnp.arange(new_dev, dtype=jnp.int32)[:, None] == target[None, :]
    arrived_rows = jnp.dot(
        placing.astype(jnp.bfloat16),
        incoming.reshape(shards * slot_cap, width_in),
        preferred_element_type=jnp.float32,
    ).astype(jnp.bfloat16)
    partial_pre = jnp.dot(arrived_rows, proj_weight, preferred_element_type=jnp.float32)
    pre_act = lax.psum(partial_pre, "mdl")
    activated = jax.nn.gelu(pre_act, approximate=False)
    inv_rms = lax.rsqrt(jnp.mean(activated * activated, axis=1, keepdims=True) + norm_eps)
    normed = (activated * inv_rms * norm_gain[None, :]).astype(jnp.bfloat16)

    def add_rows(piece):
        return jnp.dot(
            normed, piece.reshape(piece.shape[0], -1), preferred_element_type=jnp.float32
        )

    kv_heads = keyval_weight.shape[1]
    head_dim = keyval_weight.shape[2] // 2
    q_raw = add_rows(lax.all_gather(query_weight, "seq", axis=0, tiled=True))
    kv_raw = add_rows(lax.all_gather(keyval_weight, "seq", axis=0, tiled=True))
    cache_rows = cache_kv.shape[0]
    query_global = jnp.arange(new_dev, dtype=jnp.int32) * shards + device_index
    positions = cache_rows * shards + query_global
    heads_here = query_weight.shape[1] // head_dim
    group = heads_here // kv_heads
    queries = rotate(q_raw.reshape(new_dev, heads_here, head_dim), positions).astype(jnp.bfloat16)
    kv_rows = kv_raw.reshape(new_dev, kv_heads, 2 * head_dim)
    fresh = jnp.concatenate(
        [rotate(kv_rows[..., :head_dim], positions), kv_rows[..., head_dim:]], axis=-1
    ).astype(jnp.bfloat16)
    query_rows = (
        queries.reshape(new_dev, kv_heads, group, head_dim)
        .transpose(1, 0, 2, 3)
        .reshape(kv_heads, new_dev * group, head_dim)
    )
    query_pos = jnp.repeat(query_global, group)
    context = jnp.concatenate([cache_kv, fresh], axis=0)
    stride = cache_rows + new_dev
    inv_scale = 1.0 / math.sqrt(head_dim)

    def absorb(carried, key_block, visible):
        row_max, totals, accumulated = carried
        scores = (
            jnp.einsum(
                "hqd,khd->hqk",
                query_rows,
                key_block[:, :, :head_dim],
                preferred_element_type=jnp.float32,
            )
            * inv_scale
        )
        scores = jnp.where(visible[None], scores, mask_fill)
        new_max = jnp.maximum(row_max, jnp.max(scores, axis=2))
        weights = jnp.where(visible[None], jnp.exp(scores - new_max[:, :, None]), 0.0)
        factor = jnp.exp(row_max - new_max)
        totals = totals * factor + jnp.sum(weights, axis=2)
        mixed = jnp.einsum(
            "hqk,khd->hqd",
            weights.astype(jnp.bfloat16),
            key_block[:, :, head_dim:],
            preferred_element_type=jnp.float32,
        )
        accumulated = accumulated * factor[:, :, None] + mixed
        return (new_max, totals, accumulated)

    lanes = new_dev * group
    start_state = (
        jnp.full((kv_heads, lanes), mask_fill, jnp.float32),
        jnp.zeros((kv_heads, lanes), jnp.float32),
        jnp.zeros((kv_heads, lanes, head_dim), jnp.float32),
    )
    piece = lax.all_gather(context, "seq", axis=0, tiled=True)
    rows_in = piece.shape[0]
    padded_len = -(-rows_in // 128) * 128
    padded = piece
    tiles = padded_len // 128
    block_tiles = max((divisor for divisor in range(1, min(tiles, 8) + 1) if tiles % divisor == 0))
    block_len = 128 * block_tiles

    def fold_block(block_no, state_now):
        key_block = lax.dynamic_slice_in_dim(padded, block_no * block_len, block_len, 0)
        key_offset = block_no * block_len + jnp.arange(block_len, dtype=jnp.int32)
        source = key_offset // stride
        local_key = key_offset % stride
        key_global = (local_key - cache_rows) * shards + source
        present = (key_offset < rows_in)[None, :]
        visible = present & (
            (local_key < cache_rows)[None, :] | (key_global[None, :] <= query_pos[:, None])
        )
        return absorb(state_now, key_block, visible)

    row_max, totals, accumulated = lax.fori_loop(
        0, padded_len // block_len, fold_block, start_state
    )
    attended = (
        (accumulated / totals[:, :, None])
        .reshape(kv_heads, new_dev, group, head_dim)
        .transpose(1, 0, 2, 3)
    )
    attended = attended.reshape(new_dev, 1, heads_here * head_dim).astype(jnp.bfloat16)
    return (attended, fresh.reshape(new_dev, 1, kv_heads, 2 * head_dim))


MESH = pl.DeviceIdType.MESH
XS = 2


def fused_kernel(
    n,
    vis_hbm,
    target_hbm,
    counts_hbm,
    gain_hbm,
    proj_hbm,
    wq_hbm,
    wkv_hbm,
    cache_hbm,
    cos_hbm,
    sin_hbm,
    attn_ref,
    newkv_ref,
    vis_ref,
    target_ref,
    counts_ref,
    gain_ref,
    proj,
    wq,
    wkv,
    cos_t,
    sin_t,
    cache_all,
    packed,
    incoming,
    pre,
    pre_recv,
    act,
    norm_send,
    norm_all,
    part_kv,
    part_q,
    zsend_kv,
    zrecv_kv,
    zsend_q,
    zrecv_q,
    fresh_all,
    q_rows,
    load_sem,
    s_cache,
    r_cache,
    s_tok,
    r_tok,
    s_pre,
    r_pre,
    s_norm,
    r_norm,
    s_fwd,
    r_fwd,
    s_w,
    r_w,
    s_y,
    r_y,
    s_z,
    r_z,
    s_fresh,
    r_fresh,
):
    s = lax.axis_index("seq")
    m = lax.axis_index("mdl")
    zs = n // XS
    z, x = s // XS, s % XS
    g = lax.axis_index("grp")
    mate = {"mdl": 1 - m}
    beside_x = {"seq": z * XS + 1 - x}
    beside_y = {"grp": 1 - g}
    peers = [(s + k) % n for k in range(n)]

    def send(src, dst, ssem, rsem, device):
        copy = pltpu.make_async_remote_copy(
            src_ref=src,
            dst_ref=dst,
            send_sem=ssem,
            recv_sem=rsem,
            device_id=device,
            device_id_type=MESH,
        )
        copy.start()
        return copy

    barrier = pltpu.get_barrier_semaphore()
    for k in range(1, n):
        pl.semaphore_signal(barrier, inc=1, device_id={"seq": peers[k]}, device_id_type=MESH)
    pl.semaphore_signal(barrier, inc=1, device_id=mate, device_id_type=MESH)
    pl.semaphore_signal(barrier, inc=1, device_id=beside_y, device_id_type=MESH)

    loads = []
    for at, (src, dst) in enumerate(
        (
            (counts_hbm, counts_ref),
            (target_hbm, target_ref),
            (vis_hbm, vis_ref),
            (cache_hbm, cache_all.at[s]),
            (wkv_hbm, wkv.at[x]),
            (wq_hbm, wq.at[x]),
            (proj_hbm, proj),
            (cos_hbm.at[s], cos_t),
            (sin_hbm.at[s], sin_t),
            (gain_hbm, gain_ref),
        )
    ):
        copy = pltpu.make_async_copy(src, dst, load_sem.at[at])
        copy.start()
        loads.append(copy)

    toks = vis_ref.shape[1]
    cap = packed.shape[1]
    slots = n * cap
    new_dev = toks // 2
    loads[0].wait()
    prefix = []
    running = jnp.int32(0)
    here = jnp.int32(0)
    for i in range(n):
        prefix.append(running)
        here = jnp.where(s == i, running, here)
        running = running + counts_ref[i]
    slot = lax.broadcasted_iota(jnp.int32, (slots, toks), 0)
    local_row = ((slot // cap - here) & (n - 1)) + (slot % cap) * n
    loads[1].wait()
    chosen = jnp.where(local_row == target_ref[...], 1.0, 0.0)
    sizes = jnp.sum(chosen, axis=1, keepdims=True)
    loads[2].wait()
    contract = (((1,), (1,)), ((), ()))
    summed = lax.dot_general(
        chosen.astype(jnp.bfloat16), vis_ref[...], contract, preferred_element_type=jnp.float32
    )
    merged = (summed / jnp.where(sizes > 0.0, sizes, 1.0)).astype(jnp.bfloat16)
    packed[...] = merged.reshape(packed.shape)

    pl.semaphore_wait(barrier, n + 1)
    tok_copies = [
        send(packed.at[peers[k]], incoming.at[s], s_tok.at[k], r_tok.at[k], {"seq": peers[k]})
        for k in range(1, n)
    ]
    depth = wq.shape[1]
    part_rows = depth // 4
    loads[4].wait()
    loads[5].wait()
    pieces = []
    for c in range(2):
        at = pl.ds(pl.multiple_of((g * 2 + c) * part_rows, 16), part_rows)
        for which, weight in enumerate((wkv, wq)):
            pieces.append((weight.at[x, at], weight.at[1 - x, at]))
    straight = [
        send(src, src, s_w.at[at], r_w.at[at], beside_x) for at, (src, _) in enumerate(pieces)
    ]

    def pass_on(which):
        copies = []
        for at in which:
            straight[at].wait()
            dst = pieces[at][1]
            copies.append(send(dst, dst, s_y.at[at], r_y.at[at], beside_y))
        return copies

    loads[3].wait()
    cache_copies = [
        send(cache_all.at[s], cache_all.at[s], s_cache.at[k], r_cache.at[k], {"seq": peers[k]})
        for k in range(1, n)
    ]
    incoming[s] = packed[s]

    column = lax.broadcasted_iota(jnp.int32, (new_dev, slots), 1)
    source = column // cap
    starts = jnp.zeros_like(column)
    ends = jnp.zeros_like(column)
    for i in range(n):
        starts = jnp.where(source == i, prefix[i], starts)
        ends = jnp.where(source == i, prefix[i] + counts_ref[i], ends)
    global_row = starts + ((s - starts) & (n - 1)) + (column % cap) * n
    goal = jnp.where(global_row < ends, global_row // n, -1)
    placing = jnp.where(
        goal == lax.broadcasted_iota(jnp.int32, (new_dev, slots), 0), 1.0, 0.0
    ).astype(jnp.bfloat16)
    loads[6].wait()
    for copy in tok_copies:
        copy.wait()
    rows = jnp.dot(
        placing,
        incoming[...].reshape(slots, incoming.shape[2]),
        preferred_element_type=jnp.float32,
    ).astype(jnp.bfloat16)

    width = proj.shape[1]
    half = new_dev // 2
    step = 512
    mine = pl.ds(pl.multiple_of(m * half, half), half)
    other = pl.ds(pl.multiple_of((1 - m) * half, half), half)
    pre_copies = []
    for c in range(width // step):
        cols = pl.ds(c * step, step)
        pre[c] = jnp.dot(rows, proj[:, cols], preferred_element_type=jnp.float32)
        pre_copies.append(
            send(pre.at[c, other], pre_recv.at[c], s_pre.at[c], r_pre.at[c], mate)
        )
    square = jnp.zeros((half, step), jnp.float32)
    for c in range(width // step):
        pre_copies[c].wait()
        value = pre[c, mine] + pre_recv[c]
        value = 0.5 * value * (1.0 + lax.erf(value * (1.0 / math.sqrt(2.0))))
        square = square + value * value
        act[:, pl.ds(c * step, step)] = value
    mean = jnp.sum(square, axis=1, keepdims=True) / width
    inv_rms = lax.rsqrt(mean + norm_eps)
    loads[9].wait()
    lane = gain_ref.shape[1]
    normed = jnp.concatenate(
        [
            (act[:, pl.ds(j * lane, lane)] * inv_rms * gain_ref[pl.ds(j, 1), :]).astype(
                jnp.bfloat16
            )
            for j in range(width // lane)
        ],
        axis=1,
    )
    wide = width // zs
    for d in range(zs):
        norm_send[d] = normed[:, d * wide : (d + 1) * wide]
    norm_copies = []
    for k in range(1, zs):
        zt = (z + k) % zs
        norm_copies.append(
            send(
                norm_send.at[zt],
                norm_all.at[z, m],
                s_norm.at[k],
                r_norm.at[k],
                {"seq": zt * XS + x},
            )
        )
    norm_all[z, m] = norm_send[z]
    forwards = [send(norm_all.at[z, m], norm_all.at[z, m], s_fwd.at[0], r_fwd.at[0], mate)]
    crossing = pass_on((0, 1))
    for k in range(1, zs):
        norm_copies[k - 1].wait()
        came = norm_all.at[(z + zs - k) % zs, m]
        forwards.append(send(came, came, s_fwd.at[k], r_fwd.at[k], mate))
    crossing = crossing + pass_on((2, 3))
    for copy in forwards:
        copy.wait()
    for copy in crossing:
        copy.wait()

    lhs = norm_all[...].reshape(zs * new_dev, wide)
    order = [(z + k) % zs for k in range(1, zs)]

    def along_z(which, weight, part, zsend, zrecv):
        part[...] = jnp.dot(
            lhs, weight[...].reshape(wide, weight.shape[2]), preferred_element_type=jnp.float32
        ).reshape(part.shape)
        copies = []
        for k, zt in enumerate(order):
            zsend[k] = part[zt].astype(jnp.bfloat16)
            copies.append(
                send(
                    zsend.at[k],
                    zrecv.at[k],
                    s_z.at[which, k],
                    r_z.at[which, k],
                    {"seq": zt * XS + x},
                )
            )
        return part[z], copies

    def finish(total, copies, zrecv):
        for k, copy in enumerate(copies):
            copy.wait()
            total = total + zrecv[k].astype(jnp.float32)
        return total

    head = cos_t.shape[1]
    kv_own, kv_copies = along_z(0, wkv, part_kv, zsend_kv, zrecv_kv)
    q_own, q_copies = along_z(1, wq, part_q, zsend_q, zrecv_q)
    loads[7].wait()
    loads[8].wait()
    cosine, sine = cos_t[...], sin_t[...]

    def turn(value):
        return value * cosine + pltpu.roll(value, head // 2, 1) * sine

    total = finish(kv_own, kv_copies, zrecv_kv)
    fresh = jnp.concatenate([turn(total[:, :head]), total[:, head:]], axis=1).astype(jnp.bfloat16)
    fresh_all[s] = fresh
    newkv_ref[...] = fresh
    fresh_copies = [
        send(fresh_all.at[s], fresh_all.at[s], s_fresh.at[k], r_fresh.at[k], {"seq": peers[k]})
        for k in range(1, n)
    ]
    total = finish(q_own, q_copies, zrecv_q)
    heads = total.shape[1] // head
    for h in range(heads):
        q_rows[pl.ds(h * new_dev, new_dev), :] = turn(
            total[:, h * head : (h + 1) * head]
        ).astype(jnp.bfloat16)
    for copy in cache_copies:
        copy.wait()
    for copy in fresh_copies:
        copy.wait()

    kept = cache_all.shape[0] * cache_all.shape[1]
    old = cache_all[...].reshape(kept, 2 * head)
    new = fresh_all[...].reshape(n * new_dev, 2 * head)
    queries = q_rows[...]
    scale = 1.0 / math.sqrt(head)
    old_score = (
        lax.dot_general(queries, old[:, :head], contract, preferred_element_type=jnp.float32) * scale
    )
    new_score = (
        lax.dot_general(queries, new[:, :head], contract, preferred_element_type=jnp.float32) * scale
    )
    lanes = heads * new_dev
    key_at = lax.broadcasted_iota(jnp.int32, (lanes, n * new_dev), 1)
    query_at = lax.broadcasted_iota(jnp.int32, (lanes, n * new_dev), 0)
    visible = (key_at % new_dev) * n + key_at // new_dev <= (query_at % new_dev) * n + s
    new_score = jnp.where(visible, new_score, mask_fill)
    top = jnp.maximum(
        jnp.max(old_score, axis=1, keepdims=True), jnp.max(new_score, axis=1, keepdims=True)
    )
    old_weight = jnp.exp(old_score - top)
    new_weight = jnp.where(visible, jnp.exp(new_score - top), 0.0)
    totals = jnp.sum(old_weight, axis=1, keepdims=True) + jnp.sum(new_weight, axis=1, keepdims=True)
    mixed = jnp.dot(
        old_weight.astype(jnp.bfloat16), old[:, head:], preferred_element_type=jnp.float32
    ) + jnp.dot(new_weight.astype(jnp.bfloat16), new[:, head:], preferred_element_type=jnp.float32)
    attended = (mixed / totals).astype(jnp.bfloat16)
    for h in range(heads):
        attn_ref[:, pl.ds(h * head, head)] = attended[h * new_dev : (h + 1) * new_dev]


def fused_plan(
    vis_tokens,
    merge_target,
    merged_counts,
    proj_weight,
    norm_gain,
    query_weight,
    keyval_weight,
    cache_kv,
):
    n = lax.axis_size("seq")
    zs = n // XS
    toks, feat = vis_tokens.shape
    new_dev = toks // 2
    half = new_dev // 2
    cap = (new_dev + 3 * (new_dev // 3) + n - 1) // n
    width = proj_weight.shape[1]
    depth, qcols = query_weight.shape
    kvcols = keyval_weight.shape[2]
    head = kvcols // 2
    cached = cache_kv.shape[0]
    pos = (
        cached * n + np.arange(new_dev, dtype=np.float32)[None, :] * n
        + np.arange(n, dtype=np.float32)[:, None]
    ).astype(np.float32)
    freq = np.power(
        np.float32(theta_base), np.float32(-2.0) * np.arange(head // 2, dtype=np.float32) / np.float32(head)
    ).astype(np.float32)
    angles = (pos[:, :, None] * freq[None, None, :]).astype(np.float64)
    cos_table = np.concatenate([np.cos(angles)] * 2, axis=-1).astype(np.float32)
    sin_table = np.concatenate([-np.sin(angles), np.sin(angles)], axis=-1).astype(np.float32)
    bf, f32 = jnp.bfloat16, jnp.float32
    chunks = width // 512
    vm, dma = pltpu.VMEM, pltpu.SemaphoreType.DMA
    scratch = [
        vm((feat, toks), bf),
        vm((1, toks), jnp.int32),
        pltpu.SMEM((n,), jnp.int32),
        vm((width // 128, 128), f32),
        vm((feat, width), bf),
        vm((XS, depth, qcols), bf),
        vm((XS, depth, kvcols), bf),
        vm((new_dev, head), f32),
        vm((new_dev, head), f32),
        vm((n, cached, kvcols), bf),
        vm((n, cap, feat), bf),
        vm((n, cap, feat), bf),
        vm((chunks, new_dev, 512), f32),
        vm((chunks, half, 512), f32),
        vm((half, width), f32),
        vm((zs, half, depth * XS), bf),
        vm((zs, 2, half, depth * XS), bf),
        vm((zs, new_dev, kvcols), f32),
        vm((zs, new_dev, qcols), f32),
        vm((zs - 1, new_dev, kvcols), bf),
        vm((zs - 1, new_dev, kvcols), bf),
        vm((zs - 1, new_dev, qcols), bf),
        vm((zs - 1, new_dev, qcols), bf),
        vm((n, new_dev, kvcols), bf),
        vm((qcols // head * new_dev, head), bf),
        dma((10,)),
        dma((n,)),
        dma((n,)),
        dma((n,)),
        dma((n,)),
        dma((chunks,)),
        dma((chunks,)),
        dma((n,)),
        dma((n,)),
        dma((n,)),
        dma((n,)),
        dma((4,)),
        dma((4,)),
        dma((4,)),
        dma((4,)),
        dma((2, zs)),
        dma((2, zs)),
        dma((n,)),
        dma((n,)),
    ]
    in_vmem = pl.BlockSpec(memory_space=pltpu.VMEM)
    in_hbm = pl.BlockSpec(memory_space=pltpu.HBM)
    attended, fresh = pl.pallas_call(
        functools.partial(fused_kernel, n),
        out_shape=(
            jax.ShapeDtypeStruct((new_dev, qcols), bf),
            jax.ShapeDtypeStruct((new_dev, kvcols), bf),
        ),
        in_specs=[in_hbm] * 10,
        out_specs=(in_vmem, in_vmem),
        scratch_shapes=scratch,
        compiler_params=pltpu.CompilerParams(
            collective_id=0, has_side_effects=True, vmem_limit_bytes=60 * 1024 * 1024
        ),
    )(
        vis_tokens.T,
        merge_target.reshape(1, toks),
        merged_counts,
        norm_gain.reshape(width // 128, 128),
        proj_weight,
        query_weight,
        keyval_weight.reshape(depth, kvcols),
        cache_kv.reshape(cached, kvcols),
        jnp.asarray(cos_table),
        jnp.asarray(sin_table),
    )
    return (
        attended.reshape(new_dev, 1, qcols),
        fresh.reshape(new_dev, 1, keyval_weight.shape[1], kvcols),
    )


def solution(mesh):
    placed = (
        P(("grp", "seq"), "mdl"),
        P(("grp", "seq")),
        P("grp"),
        P("mdl", None),
        P(),
        P("seq", "mdl"),
        P("seq", "mdl", None),
        P(("grp", "seq"), "mdl", None),
    )
    small = mesh.shape["seq"] == 8 and mesh.shape["grp"] == 2
    per_device = fused_plan if small else plain_plan
    return jax.shard_map(
        per_device,
        mesh=mesh,
        in_specs=placed,
        out_specs=(P(None, ("grp", "seq"), "mdl"), P(None, ("grp", "seq"), "mdl", None)),
        check_vma=False,
    )
```

```python
import functools
import math

import jax
import jax.numpy as jnp
import numpy as np
from jax import lax
from jax.experimental import pallas as pl
from jax.experimental.pallas import tpu as pltpu
from jax.sharding import PartitionSpec as P

theta_base = 1000000.0
norm_eps = 1e-06
mask_fill = -1e30


def rotate(head_rows, positions):
    half_dim = head_rows.shape[-1] // 2
    frequency = jnp.power(
        theta_base, -2.0 * jnp.arange(half_dim, dtype=jnp.float32) / head_rows.shape[-1]
    )
    angles = positions.astype(jnp.float32)[:, None] * frequency[None, :]
    cosine = jnp.concatenate([jnp.cos(angles), jnp.cos(angles)], axis=-1)[:, None, :]
    sine_part = jnp.concatenate([jnp.sin(angles), jnp.sin(angles)], axis=-1)[:, None, :]
    front_half = head_rows[..., :half_dim]
    back_half = head_rows[..., half_dim:]
    turned = jnp.concatenate([-back_half, front_half], axis=-1)
    return head_rows * cosine + turned * sine_part


def plain_plan(
    vis_tokens,
    merge_target,
    merged_counts,
    proj_weight,
    norm_gain,
    query_weight,
    keyval_weight,
    cache_kv,
):
    shards = lax.axis_size("seq")
    device_index = lax.axis_index("seq")
    tok_in, width_in = vis_tokens.shape
    new_dev = tok_in // 2
    slot_cap = (new_dev + 3 * (new_dev // 3) + shards - 1) // shards
    offsets = jnp.cumsum(merged_counts) - merged_counts
    count_here = merged_counts[device_index]
    offset_here = offsets[device_index]
    slot_rows = jnp.arange(tok_in, dtype=jnp.int32)
    chosen = slot_rows[:, None] == merge_target[None, :]
    sizes = jnp.sum(chosen.astype(jnp.float32), axis=1)
    summed = jnp.dot(chosen.astype(jnp.bfloat16), vis_tokens, preferred_element_type=jnp.float32)
    merged = (summed / jnp.where(sizes > 0.0, sizes, 1.0)[:, None]).astype(jnp.bfloat16)
    peer_ids = jnp.arange(shards, dtype=jnp.int32)
    slot_ids = jnp.arange(slot_cap, dtype=jnp.int32)
    local_row = jnp.mod(peer_ids - offset_here, shards)[:, None] + slot_ids[None, :] * shards
    is_valid = local_row < count_here
    picked = jnp.take(merged, jnp.minimum(local_row, tok_in - 1).reshape(-1), axis=0).reshape(
        shards, slot_cap, width_in
    )
    outgoing = jnp.where(is_valid[:, :, None], picked, jnp.zeros_like(picked))
    incoming = lax.all_to_all(outgoing, "seq", split_axis=0, concat_axis=0, tiled=True)
    first_row = offsets + jnp.mod(device_index - offsets, shards)
    global_row = first_row[:, None] + slot_ids[None, :] * shards
    arrived = global_row < (offsets + merged_counts)[:, None]
    target = jnp.where(arrived, global_row // shards, -1).reshape(-1)
    placing = jnp.arange(new_dev, dtype=jnp.int32)[:, None] == target[None, :]
    arrived_rows = jnp.dot(
        placing.astype(jnp.bfloat16),
        incoming.reshape(shards * slot_cap, width_in),
        preferred_element_type=jnp.float32,
    ).astype(jnp.bfloat16)
    partial_pre = jnp.dot(arrived_rows, proj_weight, preferred_element_type=jnp.float32)
    pre_act = lax.psum(partial_pre, "mdl")
    activated = jax.nn.gelu(pre_act, approximate=False)
    inv_rms = lax.rsqrt(jnp.mean(activated * activated, axis=1, keepdims=True) + norm_eps)
    normed = (activated * inv_rms * norm_gain[None, :]).astype(jnp.bfloat16)

    def add_rows(piece):
        return jnp.dot(
            normed, piece.reshape(piece.shape[0], -1), preferred_element_type=jnp.float32
        )

    kv_heads = keyval_weight.shape[1]
    head_dim = keyval_weight.shape[2] // 2
    q_raw = add_rows(lax.all_gather(query_weight, "seq", axis=0, tiled=True))
    kv_raw = add_rows(lax.all_gather(keyval_weight, "seq", axis=0, tiled=True))
    cache_rows = cache_kv.shape[0]
    query_global = jnp.arange(new_dev, dtype=jnp.int32) * shards + device_index
    positions = cache_rows * shards + query_global
    heads_here = query_weight.shape[1] // head_dim
    group = heads_here // kv_heads
    queries = rotate(q_raw.reshape(new_dev, heads_here, head_dim), positions).astype(jnp.bfloat16)
    kv_rows = kv_raw.reshape(new_dev, kv_heads, 2 * head_dim)
    fresh = jnp.concatenate(
        [rotate(kv_rows[..., :head_dim], positions), kv_rows[..., head_dim:]], axis=-1
    ).astype(jnp.bfloat16)
    query_rows = (
        queries.reshape(new_dev, kv_heads, group, head_dim)
        .transpose(1, 0, 2, 3)
        .reshape(kv_heads, new_dev * group, head_dim)
    )
    query_pos = jnp.repeat(query_global, group)
    context = jnp.concatenate([cache_kv, fresh], axis=0)
    stride = cache_rows + new_dev
    inv_scale = 1.0 / math.sqrt(head_dim)

    def absorb(carried, key_block, visible):
        row_max, totals, accumulated = carried
        scores = (
            jnp.einsum(
                "hqd,khd->hqk",
                query_rows,
                key_block[:, :, :head_dim],
                preferred_element_type=jnp.float32,
            )
            * inv_scale
        )
        scores = jnp.where(visible[None], scores, mask_fill)
        new_max = jnp.maximum(row_max, jnp.max(scores, axis=2))
        weights = jnp.where(visible[None], jnp.exp(scores - new_max[:, :, None]), 0.0)
        factor = jnp.exp(row_max - new_max)
        totals = totals * factor + jnp.sum(weights, axis=2)
        mixed = jnp.einsum(
            "hqk,khd->hqd",
            weights.astype(jnp.bfloat16),
            key_block[:, :, head_dim:],
            preferred_element_type=jnp.float32,
        )
        accumulated = accumulated * factor[:, :, None] + mixed
        return (new_max, totals, accumulated)

    lanes = new_dev * group
    start_state = (
        jnp.full((kv_heads, lanes), mask_fill, jnp.float32),
        jnp.zeros((kv_heads, lanes), jnp.float32),
        jnp.zeros((kv_heads, lanes, head_dim), jnp.float32),
    )
    piece = lax.all_gather(context, "seq", axis=0, tiled=True)
    rows_in = piece.shape[0]
    padded_len = -(-rows_in // 128) * 128
    padded = piece
    tiles = padded_len // 128
    block_tiles = max((divisor for divisor in range(1, min(tiles, 8) + 1) if tiles % divisor == 0))
    block_len = 128 * block_tiles

    def fold_block(block_no, state_now):
        key_block = lax.dynamic_slice_in_dim(padded, block_no * block_len, block_len, 0)
        key_offset = block_no * block_len + jnp.arange(block_len, dtype=jnp.int32)
        source = key_offset // stride
        local_key = key_offset % stride
        key_global = (local_key - cache_rows) * shards + source
        present = (key_offset < rows_in)[None, :]
        visible = present & (
            (local_key < cache_rows)[None, :] | (key_global[None, :] <= query_pos[:, None])
        )
        return absorb(state_now, key_block, visible)

    row_max, totals, accumulated = lax.fori_loop(
        0, padded_len // block_len, fold_block, start_state
    )
    attended = (
        (accumulated / totals[:, :, None])
        .reshape(kv_heads, new_dev, group, head_dim)
        .transpose(1, 0, 2, 3)
    )
    attended = attended.reshape(new_dev, 1, heads_here * head_dim).astype(jnp.bfloat16)
    return (attended, fresh.reshape(new_dev, 1, kv_heads, 2 * head_dim))


MESH = pl.DeviceIdType.MESH
XS = 2


def fused_kernel(
    n,
    w_rows,
    vis_hbm,
    target_hbm,
    counts_hbm,
    gain_hbm,
    proj_hbm,
    wq_hbm,
    wkv_hbm,
    cache_hbm,
    cos_hbm,
    sin_hbm,
    attn_ref,
    newkv_ref,
    vis_ref,
    target_ref,
    counts_ref,
    gain_ref,
    proj,
    wq,
    wkv,
    cos_t,
    sin_t,
    cache_all,
    packed,
    incoming,
    pre,
    pre_recv,
    act,
    norm_send,
    norm_all,
    part_kv,
    part_q,
    zsend_kv,
    zrecv_kv,
    zsend_q,
    zrecv_q,
    fresh_all,
    q_rows,
    load_sem,
    s_cache,
    r_cache,
    s_tok,
    r_tok,
    s_pre,
    r_pre,
    s_norm,
    r_norm,
    s_fwd,
    r_fwd,
    s_w,
    r_w,
    s_y,
    r_y,
    s_z,
    r_z,
    s_fresh,
    r_fresh,
):
    s = lax.axis_index("seq")
    m = lax.axis_index("mdl")
    zs = n // XS
    z, x = s // XS, s % XS
    g = lax.axis_index("grp")
    mate = {"mdl": 1 - m}
    beside_x = {"seq": z * XS + 1 - x}
    beside_y = {"grp": 1 - g}
    peers = [(s + k) % n for k in range(n)]

    def send(src, dst, ssem, rsem, device):
        copy = pltpu.make_async_remote_copy(
            src_ref=src,
            dst_ref=dst,
            send_sem=ssem,
            recv_sem=rsem,
            device_id=device,
            device_id_type=MESH,
        )
        copy.start()
        return copy

    barrier = pltpu.get_barrier_semaphore()
    for k in range(1, n):
        pl.semaphore_signal(barrier, inc=1, device_id={"seq": peers[k]}, device_id_type=MESH)
    pl.semaphore_signal(barrier, inc=1, device_id=mate, device_id_type=MESH)
    pl.semaphore_signal(barrier, inc=1, device_id=beside_y, device_id_type=MESH)

    loads = []
    for at, (src, dst) in enumerate(
        (
            (counts_hbm, counts_ref),
            (target_hbm, target_ref),
            (vis_hbm, vis_ref),
            (cache_hbm, cache_all.at[s]),
            (wkv_hbm, wkv.at[x]),
            (wq_hbm, wq.at[x]),
            (proj_hbm, proj),
            (cos_hbm.at[s], cos_t),
            (sin_hbm.at[s], sin_t),
            (gain_hbm, gain_ref),
        )
    ):
        copy = pltpu.make_async_copy(src, dst, load_sem.at[at])
        copy.start()
        loads.append(copy)

    toks = vis_ref.shape[1]
    cap = packed.shape[1]
    slots = n * cap
    new_dev = toks // 2
    loads[0].wait()
    prefix = []
    running = jnp.int32(0)
    here = jnp.int32(0)
    for i in range(n):
        prefix.append(running)
        here = jnp.where(s == i, running, here)
        running = running + counts_ref[i]
    slot = lax.broadcasted_iota(jnp.int32, (slots, toks), 0)
    local_row = ((slot // cap - here) & (n - 1)) + (slot % cap) * n
    loads[1].wait()
    chosen = jnp.where(local_row == target_ref[...], 1.0, 0.0)
    sizes = jnp.sum(chosen, axis=1, keepdims=True)
    loads[2].wait()
    contract = (((1,), (1,)), ((), ()))
    summed = lax.dot_general(
        chosen.astype(jnp.bfloat16), vis_ref[...], contract, preferred_element_type=jnp.float32
    )
    merged = (summed / jnp.where(sizes > 0.0, sizes, 1.0)).astype(jnp.bfloat16)
    packed[...] = merged.reshape(packed.shape)

    pl.semaphore_wait(barrier, n + 1)
    tok_copies = [
        send(packed.at[peers[k]], incoming.at[s], s_tok.at[k], r_tok.at[k], {"seq": peers[k]})
        for k in range(1, n)
    ]
    depth = wq.shape[1]
    loads[4].wait()
    loads[5].wait()
    pieces = []
    for first, count in w_rows:
        at = pl.ds(pl.multiple_of(g * (depth // 2) + first, 16), count)
        for which, weight in enumerate((wkv, wq)):
            pieces.append((weight.at[x, at], weight.at[1 - x, at]))
    straight = [
        send(src, src, s_w.at[at], r_w.at[at], beside_x) for at, (src, _) in enumerate(pieces)
    ]

    def pass_on(which):
        copies = []
        for at in which:
            straight[at].wait()
            dst = pieces[at][1]
            copies.append(send(dst, dst, s_y.at[at], r_y.at[at], beside_y))
        return copies

    loads[3].wait()
    cache_copies = [
        send(
            cache_all.at[s],
            cache_all.at[s],
            s_cache.at[k],
            r_cache.at[k],
            {"seq": (z + k) % zs * XS + x},
        )
        for k in range(1, zs)
    ]

    def share_x(buffer, copies, ssem, rsem):
        shared = [send(buffer.at[s], buffer.at[s], ssem.at[zs], rsem.at[zs], beside_x)]
        for k in range(1, zs):
            copies[k - 1].wait()
            came = buffer.at[(z + zs - k) % zs * XS + x]
            shared.append(send(came, came, ssem.at[zs + k], rsem.at[zs + k], beside_x))
        return shared

    incoming[s] = packed[s]

    column = lax.broadcasted_iota(jnp.int32, (new_dev, slots), 1)
    source = column // cap
    starts = jnp.zeros_like(column)
    ends = jnp.zeros_like(column)
    for i in range(n):
        starts = jnp.where(source == i, prefix[i], starts)
        ends = jnp.where(source == i, prefix[i] + counts_ref[i], ends)
    global_row = starts + ((s - starts) & (n - 1)) + (column % cap) * n
    goal = jnp.where(global_row < ends, global_row // n, -1)
    placing = jnp.where(
        goal == lax.broadcasted_iota(jnp.int32, (new_dev, slots), 0), 1.0, 0.0
    ).astype(jnp.bfloat16)
    loads[6].wait()
    for copy in tok_copies:
        copy.wait()
    rows = jnp.dot(
        placing,
        incoming[...].reshape(slots, incoming.shape[2]),
        preferred_element_type=jnp.float32,
    ).astype(jnp.bfloat16)

    width = proj.shape[1]
    half = new_dev // 2
    step = 512
    mine = pl.ds(pl.multiple_of(m * half, half), half)
    other = pl.ds(pl.multiple_of((1 - m) * half, half), half)
    pre_copies = []
    for c in range(width // step):
        cols = pl.ds(c * step, step)
        pre[c] = jnp.dot(rows, proj[:, cols], preferred_element_type=jnp.float32)
        pre_copies.append(
            send(pre.at[c, other], pre_recv.at[c], s_pre.at[c], r_pre.at[c], mate)
        )
    square = jnp.zeros((half, step), jnp.float32)
    for c in range(width // step):
        pre_copies[c].wait()
        value = pre[c, mine] + pre_recv[c]
        value = 0.5 * value * (1.0 + lax.erf(value * (1.0 / math.sqrt(2.0))))
        square = square + value * value
        act[:, pl.ds(c * step, step)] = value
    mean = jnp.sum(square, axis=1, keepdims=True) / width
    inv_rms = lax.rsqrt(mean + norm_eps)
    loads[9].wait()
    lane = gain_ref.shape[1]
    normed = jnp.concatenate(
        [
            (act[:, pl.ds(j * lane, lane)] * inv_rms * gain_ref[pl.ds(j, 1), :]).astype(
                jnp.bfloat16
            )
            for j in range(width // lane)
        ],
        axis=1,
    )
    wide = width // zs
    for d in range(zs):
        norm_send[d] = normed[:, d * wide : (d + 1) * wide]
    norm_copies = []
    for k in range(1, zs):
        zt = (z + k) % zs
        norm_copies.append(
            send(
                norm_send.at[zt],
                norm_all.at[z, m],
                s_norm.at[k],
                r_norm.at[k],
                {"seq": zt * XS + x},
            )
        )
    norm_all[z, m] = norm_send[z]
    forwards = [send(norm_all.at[z, m], norm_all.at[z, m], s_fwd.at[0], r_fwd.at[0], mate)]
    early = len(pieces) // 2
    crossing = pass_on(range(early))
    for k in range(1, zs):
        norm_copies[k - 1].wait()
        came = norm_all.at[(z + zs - k) % zs, m]
        forwards.append(send(came, came, s_fwd.at[k], r_fwd.at[k], mate))
    crossing = crossing + pass_on(range(early, len(pieces)))
    for copy in forwards:
        copy.wait()
    for copy in crossing:
        copy.wait()

    lhs = norm_all[...].reshape(zs * new_dev, wide)
    order = [(z + k) % zs for k in range(1, zs)]

    def along_z(which, weight, part, zsend, zrecv):
        part[...] = jnp.dot(
            lhs, weight[...].reshape(wide, weight.shape[2]), preferred_element_type=jnp.float32
        ).reshape(part.shape)
        copies = []
        for k, zt in enumerate(order):
            zsend[k] = part[zt].astype(jnp.bfloat16)
            copies.append(
                send(
                    zsend.at[k],
                    zrecv.at[k],
                    s_z.at[which, k],
                    r_z.at[which, k],
                    {"seq": zt * XS + x},
                )
            )
        return part[z], copies

    def finish(total, copies, zrecv):
        for k, copy in enumerate(copies):
            copy.wait()
            total = total + zrecv[k].astype(jnp.float32)
        return total

    head = cos_t.shape[1]
    kv_own, kv_copies = along_z(0, wkv, part_kv, zsend_kv, zrecv_kv)
    q_own, q_copies = along_z(1, wq, part_q, zsend_q, zrecv_q)
    cache_shared = share_x(cache_all, cache_copies, s_cache, r_cache)
    loads[7].wait()
    loads[8].wait()
    cosine, sine = cos_t[...], sin_t[...]

    def turn(value):
        return value * cosine + pltpu.roll(value, head // 2, 1) * sine

    total = finish(kv_own, kv_copies, zrecv_kv)
    fresh = jnp.concatenate([turn(total[:, :head]), total[:, head:]], axis=1).astype(jnp.bfloat16)
    fresh_all[s] = fresh
    newkv_ref[...] = fresh
    fresh_copies = [
        send(
            fresh_all.at[s],
            fresh_all.at[s],
            s_fresh.at[k],
            r_fresh.at[k],
            {"seq": (z + k) % zs * XS + x},
        )
        for k in range(1, zs)
    ]
    fresh_shared = share_x(fresh_all, fresh_copies, s_fresh, r_fresh)
    total = finish(q_own, q_copies, zrecv_q)
    heads = total.shape[1] // head
    for h in range(heads):
        q_rows[pl.ds(h * new_dev, new_dev), :] = turn(
            total[:, h * head : (h + 1) * head]
        ).astype(jnp.bfloat16)
    for copy in cache_shared:
        copy.wait()
    for copy in fresh_shared:
        copy.wait()

    kept = cache_all.shape[0] * cache_all.shape[1]
    old = cache_all[...].reshape(kept, 2 * head)
    new = fresh_all[...].reshape(n * new_dev, 2 * head)
    queries = q_rows[...]
    scale = 1.0 / math.sqrt(head)
    old_score = (
        lax.dot_general(queries, old[:, :head], contract, preferred_element_type=jnp.float32) * scale
    )
    new_score = (
        lax.dot_general(queries, new[:, :head], contract, preferred_element_type=jnp.float32) * scale
    )
    lanes = heads * new_dev
    key_at = lax.broadcasted_iota(jnp.int32, (lanes, n * new_dev), 1)
    query_at = lax.broadcasted_iota(jnp.int32, (lanes, n * new_dev), 0)
    visible = (key_at % new_dev) * n + key_at // new_dev <= (query_at % new_dev) * n + s
    new_score = jnp.where(visible, new_score, mask_fill)
    top = jnp.maximum(
        jnp.max(old_score, axis=1, keepdims=True), jnp.max(new_score, axis=1, keepdims=True)
    )
    old_weight = jnp.exp(old_score - top)
    new_weight = jnp.where(visible, jnp.exp(new_score - top), 0.0)
    totals = jnp.sum(old_weight, axis=1, keepdims=True) + jnp.sum(new_weight, axis=1, keepdims=True)
    mixed = jnp.dot(
        old_weight.astype(jnp.bfloat16), old[:, head:], preferred_element_type=jnp.float32
    ) + jnp.dot(new_weight.astype(jnp.bfloat16), new[:, head:], preferred_element_type=jnp.float32)
    attended = (mixed / totals).astype(jnp.bfloat16)
    for h in range(heads):
        attn_ref[:, pl.ds(h * head, head)] = attended[h * new_dev : (h + 1) * new_dev]


def fused_plan(
    vis_tokens,
    merge_target,
    merged_counts,
    proj_weight,
    norm_gain,
    query_weight,
    keyval_weight,
    cache_kv,
):
    n = lax.axis_size("seq")
    zs = n // XS
    toks, feat = vis_tokens.shape
    new_dev = toks // 2
    half = new_dev // 2
    cap = (new_dev + 3 * (new_dev // 3) + n - 1) // n
    width = proj_weight.shape[1]
    depth, qcols = query_weight.shape
    kvcols = keyval_weight.shape[2]
    head = kvcols // 2
    cached = cache_kv.shape[0]
    pos = (
        cached * n + np.arange(new_dev, dtype=np.float32)[None, :] * n
        + np.arange(n, dtype=np.float32)[:, None]
    ).astype(np.float32)
    freq = np.power(
        np.float32(theta_base), np.float32(-2.0) * np.arange(head // 2, dtype=np.float32) / np.float32(head)
    ).astype(np.float32)
    angles = (pos[:, :, None] * freq[None, None, :]).astype(np.float64)
    cos_table = np.concatenate([np.cos(angles)] * 2, axis=-1).astype(np.float32)
    sin_table = np.concatenate([-np.sin(angles), np.sin(angles)], axis=-1).astype(np.float32)
    bf, f32 = jnp.bfloat16, jnp.float32
    chunks = width // 512
    w_rows = [(at, min(64, depth // 2 - at)) for at in range(0, depth // 2, 64)]
    pieces = 2 * len(w_rows)
    vm, dma = pltpu.VMEM, pltpu.SemaphoreType.DMA
    scratch = [
        vm((feat, toks), bf),
        vm((1, toks), jnp.int32),
        pltpu.SMEM((n,), jnp.int32),
        vm((width // 128, 128), f32),
        vm((feat, width), bf),
        vm((XS, depth, qcols), bf),
        vm((XS, depth, kvcols), bf),
        vm((new_dev, head), f32),
        vm((new_dev, head), f32),
        vm((n, cached, kvcols), bf),
        vm((n, cap, feat), bf),
        vm((n, cap, feat), bf),
        vm((chunks, new_dev, 512), f32),
        vm((chunks, half, 512), f32),
        vm((half, width), f32),
        vm((zs, half, depth * XS), bf),
        vm((zs, 2, half, depth * XS), bf),
        vm((zs, new_dev, kvcols), f32),
        vm((zs, new_dev, qcols), f32),
        vm((zs - 1, new_dev, kvcols), bf),
        vm((zs - 1, new_dev, kvcols), bf),
        vm((zs - 1, new_dev, qcols), bf),
        vm((zs - 1, new_dev, qcols), bf),
        vm((n, new_dev, kvcols), bf),
        vm((qcols // head * new_dev, head), bf),
        dma((10,)),
        dma((n,)),
        dma((n,)),
        dma((n,)),
        dma((n,)),
        dma((chunks,)),
        dma((chunks,)),
        dma((n,)),
        dma((n,)),
        dma((n,)),
        dma((n,)),
        dma((pieces,)),
        dma((pieces,)),
        dma((pieces,)),
        dma((pieces,)),
        dma((2, zs)),
        dma((2, zs)),
        dma((n,)),
        dma((n,)),
    ]
    in_vmem = pl.BlockSpec(memory_space=pltpu.VMEM)
    in_hbm = pl.BlockSpec(memory_space=pltpu.HBM)
    attended, fresh = pl.pallas_call(
        functools.partial(fused_kernel, n, w_rows),
        out_shape=(
            jax.ShapeDtypeStruct((new_dev, qcols), bf),
            jax.ShapeDtypeStruct((new_dev, kvcols), bf),
        ),
        in_specs=[in_hbm] * 10,
        out_specs=(in_vmem, in_vmem),
        scratch_shapes=scratch,
        compiler_params=pltpu.CompilerParams(
            collective_id=0, has_side_effects=True, vmem_limit_bytes=60 * 1024 * 1024
        ),
    )(
        vis_tokens.T,
        merge_target.reshape(1, toks),
        merged_counts,
        norm_gain.reshape(width // 128, 128),
        proj_weight,
        query_weight,
        keyval_weight.reshape(depth, kvcols),
        cache_kv.reshape(cached, kvcols),
        jnp.asarray(cos_table),
        jnp.asarray(sin_table),
    )
    return (
        attended.reshape(new_dev, 1, qcols),
        fresh.reshape(new_dev, 1, keyval_weight.shape[1], kvcols),
    )


def solution(mesh):
    placed = (
        P(("grp", "seq"), "mdl"),
        P(("grp", "seq")),
        P("grp"),
        P("mdl", None),
        P(),
        P("seq", "mdl"),
        P("seq", "mdl", None),
        P(("grp", "seq"), "mdl", None),
    )
    small = mesh.shape["seq"] == 8 and mesh.shape["grp"] == 2
    per_device = fused_plan if small else plain_plan
    return jax.shard_map(
        per_device,
        mesh=mesh,
        in_specs=placed,
        out_specs=(P(None, ("grp", "seq"), "mdl"), P(None, ("grp", "seq"), "mdl", None)),
        check_vma=False,
    )
```

```python
import functools
import math

import jax
import jax.numpy as jnp
import numpy as np
from jax import lax
from jax.experimental import pallas as pl
from jax.experimental.pallas import tpu as pltpu
from jax.sharding import PartitionSpec as P

theta_base = 1000000.0
norm_eps = 1e-06
mask_fill = -1e30


def rotate(head_rows, positions):
    half_dim = head_rows.shape[-1] // 2
    frequency = jnp.power(
        theta_base, -2.0 * jnp.arange(half_dim, dtype=jnp.float32) / head_rows.shape[-1]
    )
    angles = positions.astype(jnp.float32)[:, None] * frequency[None, :]
    cosine = jnp.concatenate([jnp.cos(angles), jnp.cos(angles)], axis=-1)[:, None, :]
    sine_part = jnp.concatenate([jnp.sin(angles), jnp.sin(angles)], axis=-1)[:, None, :]
    front_half = head_rows[..., :half_dim]
    back_half = head_rows[..., half_dim:]
    turned = jnp.concatenate([-back_half, front_half], axis=-1)
    return head_rows * cosine + turned * sine_part


def plain_plan(
    vis_tokens,
    merge_target,
    merged_counts,
    proj_weight,
    norm_gain,
    query_weight,
    keyval_weight,
    cache_kv,
):
    shards = lax.axis_size("seq")
    device_index = lax.axis_index("seq")
    tok_in, width_in = vis_tokens.shape
    new_dev = tok_in // 2
    slot_cap = (new_dev + 3 * (new_dev // 3) + shards - 1) // shards
    offsets = jnp.cumsum(merged_counts) - merged_counts
    count_here = merged_counts[device_index]
    offset_here = offsets[device_index]
    slot_rows = jnp.arange(tok_in, dtype=jnp.int32)
    chosen = slot_rows[:, None] == merge_target[None, :]
    sizes = jnp.sum(chosen.astype(jnp.float32), axis=1)
    summed = jnp.dot(chosen.astype(jnp.bfloat16), vis_tokens, preferred_element_type=jnp.float32)
    merged = (summed / jnp.where(sizes > 0.0, sizes, 1.0)[:, None]).astype(jnp.bfloat16)
    peer_ids = jnp.arange(shards, dtype=jnp.int32)
    slot_ids = jnp.arange(slot_cap, dtype=jnp.int32)
    local_row = jnp.mod(peer_ids - offset_here, shards)[:, None] + slot_ids[None, :] * shards
    is_valid = local_row < count_here
    picked = jnp.take(merged, jnp.minimum(local_row, tok_in - 1).reshape(-1), axis=0).reshape(
        shards, slot_cap, width_in
    )
    outgoing = jnp.where(is_valid[:, :, None], picked, jnp.zeros_like(picked))
    incoming = lax.all_to_all(outgoing, "seq", split_axis=0, concat_axis=0, tiled=True)
    first_row = offsets + jnp.mod(device_index - offsets, shards)
    global_row = first_row[:, None] + slot_ids[None, :] * shards
    arrived = global_row < (offsets + merged_counts)[:, None]
    target = jnp.where(arrived, global_row // shards, -1).reshape(-1)
    placing = jnp.arange(new_dev, dtype=jnp.int32)[:, None] == target[None, :]
    arrived_rows = jnp.dot(
        placing.astype(jnp.bfloat16),
        incoming.reshape(shards * slot_cap, width_in),
        preferred_element_type=jnp.float32,
    ).astype(jnp.bfloat16)
    partial_pre = jnp.dot(arrived_rows, proj_weight, preferred_element_type=jnp.float32)
    pre_act = lax.psum(partial_pre, "mdl")
    activated = jax.nn.gelu(pre_act, approximate=False)
    inv_rms = lax.rsqrt(jnp.mean(activated * activated, axis=1, keepdims=True) + norm_eps)
    normed = (activated * inv_rms * norm_gain[None, :]).astype(jnp.bfloat16)

    def add_rows(piece):
        return jnp.dot(
            normed, piece.reshape(piece.shape[0], -1), preferred_element_type=jnp.float32
        )

    kv_heads = keyval_weight.shape[1]
    head_dim = keyval_weight.shape[2] // 2
    q_raw = add_rows(lax.all_gather(query_weight, "seq", axis=0, tiled=True))
    kv_raw = add_rows(lax.all_gather(keyval_weight, "seq", axis=0, tiled=True))
    cache_rows = cache_kv.shape[0]
    query_global = jnp.arange(new_dev, dtype=jnp.int32) * shards + device_index
    positions = cache_rows * shards + query_global
    heads_here = query_weight.shape[1] // head_dim
    group = heads_here // kv_heads
    queries = rotate(q_raw.reshape(new_dev, heads_here, head_dim), positions).astype(jnp.bfloat16)
    kv_rows = kv_raw.reshape(new_dev, kv_heads, 2 * head_dim)
    fresh = jnp.concatenate(
        [rotate(kv_rows[..., :head_dim], positions), kv_rows[..., head_dim:]], axis=-1
    ).astype(jnp.bfloat16)
    query_rows = (
        queries.reshape(new_dev, kv_heads, group, head_dim)
        .transpose(1, 0, 2, 3)
        .reshape(kv_heads, new_dev * group, head_dim)
    )
    query_pos = jnp.repeat(query_global, group)
    context = jnp.concatenate([cache_kv, fresh], axis=0)
    stride = cache_rows + new_dev
    inv_scale = 1.0 / math.sqrt(head_dim)

    def absorb(carried, key_block, visible):
        row_max, totals, accumulated = carried
        scores = (
            jnp.einsum(
                "hqd,khd->hqk",
                query_rows,
                key_block[:, :, :head_dim],
                preferred_element_type=jnp.float32,
            )
            * inv_scale
        )
        scores = jnp.where(visible[None], scores, mask_fill)
        new_max = jnp.maximum(row_max, jnp.max(scores, axis=2))
        weights = jnp.where(visible[None], jnp.exp(scores - new_max[:, :, None]), 0.0)
        factor = jnp.exp(row_max - new_max)
        totals = totals * factor + jnp.sum(weights, axis=2)
        mixed = jnp.einsum(
            "hqk,khd->hqd",
            weights.astype(jnp.bfloat16),
            key_block[:, :, head_dim:],
            preferred_element_type=jnp.float32,
        )
        accumulated = accumulated * factor[:, :, None] + mixed
        return (new_max, totals, accumulated)

    lanes = new_dev * group
    start_state = (
        jnp.full((kv_heads, lanes), mask_fill, jnp.float32),
        jnp.zeros((kv_heads, lanes), jnp.float32),
        jnp.zeros((kv_heads, lanes, head_dim), jnp.float32),
    )
    piece = lax.all_gather(context, "seq", axis=0, tiled=True)
    rows_in = piece.shape[0]
    padded_len = -(-rows_in // 128) * 128
    padded = piece
    tiles = padded_len // 128
    block_tiles = max((divisor for divisor in range(1, min(tiles, 8) + 1) if tiles % divisor == 0))
    block_len = 128 * block_tiles

    def fold_block(block_no, state_now):
        key_block = lax.dynamic_slice_in_dim(padded, block_no * block_len, block_len, 0)
        key_offset = block_no * block_len + jnp.arange(block_len, dtype=jnp.int32)
        source = key_offset // stride
        local_key = key_offset % stride
        key_global = (local_key - cache_rows) * shards + source
        present = (key_offset < rows_in)[None, :]
        visible = present & (
            (local_key < cache_rows)[None, :] | (key_global[None, :] <= query_pos[:, None])
        )
        return absorb(state_now, key_block, visible)

    row_max, totals, accumulated = lax.fori_loop(
        0, padded_len // block_len, fold_block, start_state
    )
    attended = (
        (accumulated / totals[:, :, None])
        .reshape(kv_heads, new_dev, group, head_dim)
        .transpose(1, 0, 2, 3)
    )
    attended = attended.reshape(new_dev, 1, heads_here * head_dim).astype(jnp.bfloat16)
    return (attended, fresh.reshape(new_dev, 1, kv_heads, 2 * head_dim))


MESH = pl.DeviceIdType.MESH
XS = 2


def fused_kernel(
    n,
    w_rows,
    vis_hbm,
    target_hbm,
    counts_hbm,
    gain_hbm,
    proj_hbm,
    wq_hbm,
    wkv_hbm,
    cache_hbm,
    cos_hbm,
    sin_hbm,
    attn_ref,
    newkv_ref,
    vis_ref,
    target_ref,
    counts_ref,
    gain_ref,
    proj,
    wq,
    wkv,
    cos_t,
    sin_t,
    cache_all,
    packed,
    incoming,
    pre,
    pre_recv,
    act,
    norm_send,
    norm_all,
    part_kv,
    part_q,
    zsend_kv,
    zrecv_kv,
    zsend_q,
    zrecv_q,
    fresh_all,
    q_rows,
    load_sem,
    s_cache,
    r_cache,
    s_tok,
    r_tok,
    s_pre,
    r_pre,
    s_norm,
    r_norm,
    s_fwd,
    r_fwd,
    s_w,
    r_w,
    s_y,
    r_y,
    s_z,
    r_z,
    s_fresh,
    r_fresh,
):
    s = lax.axis_index("seq")
    m = lax.axis_index("mdl")
    zs = n // XS
    z, x = s // XS, s % XS
    g = lax.axis_index("grp")
    mate = {"mdl": 1 - m}
    beside_x = {"seq": z * XS + 1 - x}
    beside_y = {"grp": 1 - g}
    peers = [(s + k) % n for k in range(n)]

    def send(src, dst, ssem, rsem, device):
        copy = pltpu.make_async_remote_copy(
            src_ref=src,
            dst_ref=dst,
            send_sem=ssem,
            recv_sem=rsem,
            device_id=device,
            device_id_type=MESH,
        )
        copy.start()
        return copy

    barrier = pltpu.get_barrier_semaphore()
    for k in range(1, n):
        pl.semaphore_signal(barrier, inc=1, device_id={"seq": peers[k]}, device_id_type=MESH)
    pl.semaphore_signal(barrier, inc=1, device_id=mate, device_id_type=MESH)
    pl.semaphore_signal(barrier, inc=1, device_id=beside_y, device_id_type=MESH)

    loads = []
    for at, (src, dst) in enumerate(
        (
            (counts_hbm, counts_ref),
            (target_hbm, target_ref),
            (vis_hbm, vis_ref),
            (cache_hbm, cache_all.at[s]),
            (wkv_hbm, wkv.at[x]),
            (wq_hbm, wq.at[x]),
            (proj_hbm, proj),
            (cos_hbm.at[s], cos_t),
            (sin_hbm.at[s], sin_t),
            (gain_hbm, gain_ref),
        )
    ):
        copy = pltpu.make_async_copy(src, dst, load_sem.at[at])
        copy.start()
        loads.append(copy)

    toks = vis_ref.shape[1]
    cap = packed.shape[1]
    slots = n * cap
    new_dev = toks // 2
    loads[0].wait()
    prefix = []
    running = jnp.int32(0)
    here = jnp.int32(0)
    for i in range(n):
        prefix.append(running)
        here = jnp.where(s == i, running, here)
        running = running + counts_ref[i]
    slot = lax.broadcasted_iota(jnp.int32, (slots, toks), 0)
    local_row = ((slot // cap - here) & (n - 1)) + (slot % cap) * n
    loads[1].wait()
    chosen = jnp.where(local_row == target_ref[...], 1.0, 0.0)
    sizes = jnp.sum(chosen, axis=1, keepdims=True)
    loads[2].wait()
    contract = (((1,), (1,)), ((), ()))
    summed = lax.dot_general(
        chosen.astype(jnp.bfloat16), vis_ref[...], contract, preferred_element_type=jnp.float32
    )
    merged = (summed / jnp.where(sizes > 0.0, sizes, 1.0)).astype(jnp.bfloat16)
    packed[...] = merged.reshape(packed.shape)

    pl.semaphore_wait(barrier, n + 1)
    tok_copies = [
        send(packed.at[peers[k]], incoming.at[s], s_tok.at[k], r_tok.at[k], {"seq": peers[k]})
        for k in range(1, n)
    ]
    depth = wq.shape[1]
    loads[4].wait()
    loads[5].wait()
    pieces = []
    for weight, first, count in [(wkv, 0, depth // 2)] + [(wq, *rows) for rows in w_rows]:
        at = pl.ds(pl.multiple_of(g * (depth // 2) + first, 16), count)
        pieces.append((weight.at[x, at], weight.at[1 - x, at]))
    straight = [
        send(src, src, s_w.at[at], r_w.at[at], beside_x) for at, (src, _) in enumerate(pieces)
    ]

    def pass_on(which):
        copies = []
        for at in which:
            straight[at].wait()
            dst = pieces[at][1]
            copies.append(send(dst, dst, s_y.at[at], r_y.at[at], beside_y))
        return copies

    loads[3].wait()
    cache_copies = [
        send(
            cache_all.at[s],
            cache_all.at[s],
            s_cache.at[k],
            r_cache.at[k],
            {"seq": (z + k) % zs * XS + x},
        )
        for k in range(1, zs)
    ]

    def share_x(buffer, copies, ssem, rsem):
        shared = [send(buffer.at[s], buffer.at[s], ssem.at[zs], rsem.at[zs], beside_x)]
        for k in range(1, zs):
            copies[k - 1].wait()
            came = buffer.at[(z + zs - k) % zs * XS + x]
            shared.append(send(came, came, ssem.at[zs + k], rsem.at[zs + k], beside_x))
        return shared

    incoming[s] = packed[s]

    column = lax.broadcasted_iota(jnp.int32, (new_dev, slots), 1)
    source = column // cap
    starts = jnp.zeros_like(column)
    ends = jnp.zeros_like(column)
    for i in range(n):
        starts = jnp.where(source == i, prefix[i], starts)
        ends = jnp.where(source == i, prefix[i] + counts_ref[i], ends)
    global_row = starts + ((s - starts) & (n - 1)) + (column % cap) * n
    goal = jnp.where(global_row < ends, global_row // n, -1)
    placing = jnp.where(
        goal == lax.broadcasted_iota(jnp.int32, (new_dev, slots), 0), 1.0, 0.0
    ).astype(jnp.bfloat16)
    loads[6].wait()
    for copy in tok_copies:
        copy.wait()
    rows = jnp.dot(
        placing,
        incoming[...].reshape(slots, incoming.shape[2]),
        preferred_element_type=jnp.float32,
    ).astype(jnp.bfloat16)

    width = proj.shape[1]
    half = new_dev // 2
    step = 512
    mine = pl.ds(pl.multiple_of(m * half, half), half)
    other = pl.ds(pl.multiple_of((1 - m) * half, half), half)
    pre_copies = []
    for c in range(width // step):
        cols = pl.ds(c * step, step)
        pre[c] = jnp.dot(rows, proj[:, cols], preferred_element_type=jnp.float32)
        pre_copies.append(
            send(pre.at[c, other], pre_recv.at[c], s_pre.at[c], r_pre.at[c], mate)
        )
    square = jnp.zeros((half, step), jnp.float32)
    for c in range(width // step):
        pre_copies[c].wait()
        value = pre[c, mine] + pre_recv[c]
        value = 0.5 * value * (1.0 + lax.erf(value * (1.0 / math.sqrt(2.0))))
        square = square + value * value
        act[:, pl.ds(c * step, step)] = value
    mean = jnp.sum(square, axis=1, keepdims=True) / width
    inv_rms = lax.rsqrt(mean + norm_eps)
    loads[9].wait()
    lane = gain_ref.shape[1]
    normed = jnp.concatenate(
        [
            (act[:, pl.ds(j * lane, lane)] * inv_rms * gain_ref[pl.ds(j, 1), :]).astype(
                jnp.bfloat16
            )
            for j in range(width // lane)
        ],
        axis=1,
    )
    wide = width // zs
    for d in range(zs):
        norm_send[d] = normed[:, d * wide : (d + 1) * wide]
    norm_copies = []
    for k in range(1, zs):
        zt = (z + k) % zs
        norm_copies.append(
            send(
                norm_send.at[zt],
                norm_all.at[z, m],
                s_norm.at[k],
                r_norm.at[k],
                {"seq": zt * XS + x},
            )
        )
    norm_all[z, m] = norm_send[z]
    forwards = [send(norm_all.at[z, m], norm_all.at[z, m], s_fwd.at[0], r_fwd.at[0], mate)]
    early = 1 + len(pieces) // 2
    crossing = pass_on(range(early))
    for k in range(1, zs):
        norm_copies[k - 1].wait()
        came = norm_all.at[(z + zs - k) % zs, m]
        forwards.append(send(came, came, s_fwd.at[k], r_fwd.at[k], mate))
    crossing = crossing + pass_on(range(early, len(pieces)))
    for copy in forwards:
        copy.wait()
    crossing[0].wait()

    lhs = norm_all[...].reshape(zs * new_dev, wide)
    order = [(z + k) % zs for k in range(1, zs)]

    def along_z(which, weight, part, zsend, zrecv):
        part[...] = jnp.dot(
            lhs, weight[...].reshape(wide, weight.shape[2]), preferred_element_type=jnp.float32
        ).reshape(part.shape)
        copies = []
        for k, zt in enumerate(order):
            zsend[k] = part[zt].astype(jnp.bfloat16)
            copies.append(
                send(
                    zsend.at[k],
                    zrecv.at[k],
                    s_z.at[which, k],
                    r_z.at[which, k],
                    {"seq": zt * XS + x},
                )
            )
        return part[z], copies

    def finish(total, copies, zrecv):
        for k, copy in enumerate(copies):
            copy.wait()
            total = total + zrecv[k].astype(jnp.float32)
        return total

    head = cos_t.shape[1]
    kv_own, kv_copies = along_z(0, wkv, part_kv, zsend_kv, zrecv_kv)
    cache_shared = share_x(cache_all, cache_copies, s_cache, r_cache)
    loads[7].wait()
    loads[8].wait()
    cosine, sine = cos_t[...], sin_t[...]

    def turn(value):
        return value * cosine + pltpu.roll(value, head // 2, 1) * sine

    total = finish(kv_own, kv_copies, zrecv_kv)
    fresh = jnp.concatenate([turn(total[:, :head]), total[:, head:]], axis=1).astype(jnp.bfloat16)
    fresh_all[s] = fresh
    newkv_ref[...] = fresh
    fresh_copies = [
        send(
            fresh_all.at[s],
            fresh_all.at[s],
            s_fresh.at[k],
            r_fresh.at[k],
            {"seq": (z + k) % zs * XS + x},
        )
        for k in range(1, zs)
    ]
    for copy in crossing[1:]:
        copy.wait()
    q_own, q_copies = along_z(1, wq, part_q, zsend_q, zrecv_q)
    fresh_shared = share_x(fresh_all, fresh_copies, s_fresh, r_fresh)
    total = finish(q_own, q_copies, zrecv_q)
    heads = total.shape[1] // head
    for h in range(heads):
        q_rows[pl.ds(h * new_dev, new_dev), :] = turn(
            total[:, h * head : (h + 1) * head]
        ).astype(jnp.bfloat16)
    for copy in cache_shared:
        copy.wait()
    for copy in fresh_shared:
        copy.wait()

    kept = cache_all.shape[0] * cache_all.shape[1]
    old = cache_all[...].reshape(kept, 2 * head)
    new = fresh_all[...].reshape(n * new_dev, 2 * head)
    queries = q_rows[...]
    scale = 1.0 / math.sqrt(head)
    old_score = (
        lax.dot_general(queries, old[:, :head], contract, preferred_element_type=jnp.float32) * scale
    )
    new_score = (
        lax.dot_general(queries, new[:, :head], contract, preferred_element_type=jnp.float32) * scale
    )
    lanes = heads * new_dev
    key_at = lax.broadcasted_iota(jnp.int32, (lanes, n * new_dev), 1)
    query_at = lax.broadcasted_iota(jnp.int32, (lanes, n * new_dev), 0)
    visible = (key_at % new_dev) * n + key_at // new_dev <= (query_at % new_dev) * n + s
    new_score = jnp.where(visible, new_score, mask_fill)
    top = jnp.maximum(
        jnp.max(old_score, axis=1, keepdims=True), jnp.max(new_score, axis=1, keepdims=True)
    )
    old_weight = jnp.exp(old_score - top)
    new_weight = jnp.where(visible, jnp.exp(new_score - top), 0.0)
    totals = jnp.sum(old_weight, axis=1, keepdims=True) + jnp.sum(new_weight, axis=1, keepdims=True)
    mixed = jnp.dot(
        old_weight.astype(jnp.bfloat16), old[:, head:], preferred_element_type=jnp.float32
    ) + jnp.dot(new_weight.astype(jnp.bfloat16), new[:, head:], preferred_element_type=jnp.float32)
    attended = (mixed / totals).astype(jnp.bfloat16)
    for h in range(heads):
        attn_ref[:, pl.ds(h * head, head)] = attended[h * new_dev : (h + 1) * new_dev]


def fused_plan(
    vis_tokens,
    merge_target,
    merged_counts,
    proj_weight,
    norm_gain,
    query_weight,
    keyval_weight,
    cache_kv,
):
    n = lax.axis_size("seq")
    zs = n // XS
    toks, feat = vis_tokens.shape
    new_dev = toks // 2
    half = new_dev // 2
    cap = (new_dev + 3 * (new_dev // 3) + n - 1) // n
    width = proj_weight.shape[1]
    depth, qcols = query_weight.shape
    kvcols = keyval_weight.shape[2]
    head = kvcols // 2
    cached = cache_kv.shape[0]
    pos = (
        cached * n + np.arange(new_dev, dtype=np.float32)[None, :] * n
        + np.arange(n, dtype=np.float32)[:, None]
    ).astype(np.float32)
    freq = np.power(
        np.float32(theta_base), np.float32(-2.0) * np.arange(head // 2, dtype=np.float32) / np.float32(head)
    ).astype(np.float32)
    angles = (pos[:, :, None] * freq[None, None, :]).astype(np.float64)
    cos_table = np.concatenate([np.cos(angles)] * 2, axis=-1).astype(np.float32)
    sin_table = np.concatenate([-np.sin(angles), np.sin(angles)], axis=-1).astype(np.float32)
    bf, f32 = jnp.bfloat16, jnp.float32
    chunks = width // 512
    w_rows = [(at, min(64, depth // 2 - at)) for at in range(0, depth // 2, 64)]
    pieces = 1 + len(w_rows)
    vm, dma = pltpu.VMEM, pltpu.SemaphoreType.DMA
    scratch = [
        vm((feat, toks), bf),
        vm((1, toks), jnp.int32),
        pltpu.SMEM((n,), jnp.int32),
        vm((width // 128, 128), f32),
        vm((feat, width), bf),
        vm((XS, depth, qcols), bf),
        vm((XS, depth, kvcols), bf),
        vm((new_dev, head), f32),
        vm((new_dev, head), f32),
        vm((n, cached, kvcols), bf),
        vm((n, cap, feat), bf),
        vm((n, cap, feat), bf),
        vm((chunks, new_dev, 512), f32),
        vm((chunks, half, 512), f32),
        vm((half, width), f32),
        vm((zs, half, depth * XS), bf),
        vm((zs, 2, half, depth * XS), bf),
        vm((zs, new_dev, kvcols), f32),
        vm((zs, new_dev, qcols), f32),
        vm((zs - 1, new_dev, kvcols), bf),
        vm((zs - 1, new_dev, kvcols), bf),
        vm((zs - 1, new_dev, qcols), bf),
        vm((zs - 1, new_dev, qcols), bf),
        vm((n, new_dev, kvcols), bf),
        vm((qcols // head * new_dev, head), bf),
        dma((10,)),
        dma((n,)),
        dma((n,)),
        dma((n,)),
        dma((n,)),
        dma((chunks,)),
        dma((chunks,)),
        dma((n,)),
        dma((n,)),
        dma((n,)),
        dma((n,)),
        dma((pieces,)),
        dma((pieces,)),
        dma((pieces,)),
        dma((pieces,)),
        dma((2, zs)),
        dma((2, zs)),
        dma((n,)),
        dma((n,)),
    ]
    in_vmem = pl.BlockSpec(memory_space=pltpu.VMEM)
    in_hbm = pl.BlockSpec(memory_space=pltpu.HBM)
    attended, fresh = pl.pallas_call(
        functools.partial(fused_kernel, n, w_rows),
        out_shape=(
            pltpu.VMEM((new_dev, qcols), bf),
            pltpu.VMEM((new_dev, kvcols), bf),
        ),
        in_specs=[in_hbm] * 10,
        out_specs=(in_vmem, in_vmem),
        scratch_shapes=scratch,
        compiler_params=pltpu.CompilerParams(
            collective_id=0, has_side_effects=True, vmem_limit_bytes=60 * 1024 * 1024
        ),
    )(
        vis_tokens.T,
        merge_target.reshape(1, toks),
        merged_counts,
        norm_gain.reshape(width // 128, 128),
        proj_weight,
        query_weight,
        keyval_weight.reshape(depth, kvcols),
        cache_kv.reshape(cached, kvcols),
        jnp.asarray(cos_table),
        jnp.asarray(sin_table),
    )
    return (
        attended.reshape(new_dev, 1, qcols),
        fresh.reshape(new_dev, 1, keyval_weight.shape[1], kvcols),
    )


def solution(mesh):
    placed = (
        P(("grp", "seq"), "mdl"),
        P(("grp", "seq")),
        P("grp"),
        P("mdl", None),
        P(),
        P("seq", "mdl"),
        P("seq", "mdl", None),
        P(("grp", "seq"), "mdl", None),
    )
    small = mesh.shape["seq"] == 8 and mesh.shape["grp"] == 2
    per_device = fused_plan if small else plain_plan
    return jax.shard_map(
        per_device,
        mesh=mesh,
        in_specs=placed,
        out_specs=(P(None, ("grp", "seq"), "mdl"), P(None, ("grp", "seq"), "mdl", None)),
        check_vma=False,
    )
```

```python
import functools
import math

import jax
import jax.numpy as jnp
import numpy as np
from jax import lax
from jax.experimental import pallas as pl
from jax.experimental.pallas import tpu as pltpu
from jax.sharding import PartitionSpec as P

theta_base = 1000000.0
norm_eps = 1e-06
mask_fill = -1e30


def rotate(head_rows, positions):
    half_dim = head_rows.shape[-1] // 2
    frequency = jnp.power(
        theta_base, -2.0 * jnp.arange(half_dim, dtype=jnp.float32) / head_rows.shape[-1]
    )
    angles = positions.astype(jnp.float32)[:, None] * frequency[None, :]
    cosine = jnp.concatenate([jnp.cos(angles), jnp.cos(angles)], axis=-1)[:, None, :]
    sine_part = jnp.concatenate([jnp.sin(angles), jnp.sin(angles)], axis=-1)[:, None, :]
    front_half = head_rows[..., :half_dim]
    back_half = head_rows[..., half_dim:]
    turned = jnp.concatenate([-back_half, front_half], axis=-1)
    return head_rows * cosine + turned * sine_part


def plain_plan(
    vis_tokens,
    merge_target,
    merged_counts,
    proj_weight,
    norm_gain,
    query_weight,
    keyval_weight,
    cache_kv,
):
    shards = lax.axis_size("seq")
    device_index = lax.axis_index("seq")
    tok_in, width_in = vis_tokens.shape
    new_dev = tok_in // 2
    slot_cap = (new_dev + 3 * (new_dev // 3) + shards - 1) // shards
    offsets = jnp.cumsum(merged_counts) - merged_counts
    count_here = merged_counts[device_index]
    offset_here = offsets[device_index]
    slot_rows = jnp.arange(tok_in, dtype=jnp.int32)
    chosen = slot_rows[:, None] == merge_target[None, :]
    sizes = jnp.sum(chosen.astype(jnp.float32), axis=1)
    summed = jnp.dot(chosen.astype(jnp.bfloat16), vis_tokens, preferred_element_type=jnp.float32)
    merged = (summed / jnp.where(sizes > 0.0, sizes, 1.0)[:, None]).astype(jnp.bfloat16)
    peer_ids = jnp.arange(shards, dtype=jnp.int32)
    slot_ids = jnp.arange(slot_cap, dtype=jnp.int32)
    local_row = jnp.mod(peer_ids - offset_here, shards)[:, None] + slot_ids[None, :] * shards
    is_valid = local_row < count_here
    picked = jnp.take(merged, jnp.minimum(local_row, tok_in - 1).reshape(-1), axis=0).reshape(
        shards, slot_cap, width_in
    )
    outgoing = jnp.where(is_valid[:, :, None], picked, jnp.zeros_like(picked))
    incoming = lax.all_to_all(outgoing, "seq", split_axis=0, concat_axis=0, tiled=True)
    first_row = offsets + jnp.mod(device_index - offsets, shards)
    global_row = first_row[:, None] + slot_ids[None, :] * shards
    arrived = global_row < (offsets + merged_counts)[:, None]
    target = jnp.where(arrived, global_row // shards, -1).reshape(-1)
    placing = jnp.arange(new_dev, dtype=jnp.int32)[:, None] == target[None, :]
    arrived_rows = jnp.dot(
        placing.astype(jnp.bfloat16),
        incoming.reshape(shards * slot_cap, width_in),
        preferred_element_type=jnp.float32,
    ).astype(jnp.bfloat16)
    partial_pre = jnp.dot(arrived_rows, proj_weight, preferred_element_type=jnp.float32)
    pre_act = lax.psum(partial_pre, "mdl")
    activated = jax.nn.gelu(pre_act, approximate=False)
    inv_rms = lax.rsqrt(jnp.mean(activated * activated, axis=1, keepdims=True) + norm_eps)
    normed = (activated * inv_rms * norm_gain[None, :]).astype(jnp.bfloat16)

    def add_rows(piece):
        return jnp.dot(
            normed, piece.reshape(piece.shape[0], -1), preferred_element_type=jnp.float32
        )

    kv_heads = keyval_weight.shape[1]
    head_dim = keyval_weight.shape[2] // 2
    q_raw = add_rows(lax.all_gather(query_weight, "seq", axis=0, tiled=True))
    kv_raw = add_rows(lax.all_gather(keyval_weight, "seq", axis=0, tiled=True))
    cache_rows = cache_kv.shape[0]
    query_global = jnp.arange(new_dev, dtype=jnp.int32) * shards + device_index
    positions = cache_rows * shards + query_global
    heads_here = query_weight.shape[1] // head_dim
    group = heads_here // kv_heads
    queries = rotate(q_raw.reshape(new_dev, heads_here, head_dim), positions).astype(jnp.bfloat16)
    kv_rows = kv_raw.reshape(new_dev, kv_heads, 2 * head_dim)
    fresh = jnp.concatenate(
        [rotate(kv_rows[..., :head_dim], positions), kv_rows[..., head_dim:]], axis=-1
    ).astype(jnp.bfloat16)
    query_rows = (
        queries.reshape(new_dev, kv_heads, group, head_dim)
        .transpose(1, 0, 2, 3)
        .reshape(kv_heads, new_dev * group, head_dim)
    )
    query_pos = jnp.repeat(query_global, group)
    context = jnp.concatenate([cache_kv, fresh], axis=0)
    stride = cache_rows + new_dev
    inv_scale = 1.0 / math.sqrt(head_dim)

    def absorb(carried, key_block, visible):
        row_max, totals, accumulated = carried
        scores = (
            jnp.einsum(
                "hqd,khd->hqk",
                query_rows,
                key_block[:, :, :head_dim],
                preferred_element_type=jnp.float32,
            )
            * inv_scale
        )
        scores = jnp.where(visible[None], scores, mask_fill)
        new_max = jnp.maximum(row_max, jnp.max(scores, axis=2))
        weights = jnp.where(visible[None], jnp.exp(scores - new_max[:, :, None]), 0.0)
        factor = jnp.exp(row_max - new_max)
        totals = totals * factor + jnp.sum(weights, axis=2)
        mixed = jnp.einsum(
            "hqk,khd->hqd",
            weights.astype(jnp.bfloat16),
            key_block[:, :, head_dim:],
            preferred_element_type=jnp.float32,
        )
        accumulated = accumulated * factor[:, :, None] + mixed
        return (new_max, totals, accumulated)

    lanes = new_dev * group
    start_state = (
        jnp.full((kv_heads, lanes), mask_fill, jnp.float32),
        jnp.zeros((kv_heads, lanes), jnp.float32),
        jnp.zeros((kv_heads, lanes, head_dim), jnp.float32),
    )
    piece = lax.all_gather(context, "seq", axis=0, tiled=True)
    rows_in = piece.shape[0]
    padded_len = -(-rows_in // 128) * 128
    padded = piece
    tiles = padded_len // 128
    block_tiles = max((divisor for divisor in range(1, min(tiles, 8) + 1) if tiles % divisor == 0))
    block_len = 128 * block_tiles

    def fold_block(block_no, state_now):
        key_block = lax.dynamic_slice_in_dim(padded, block_no * block_len, block_len, 0)
        key_offset = block_no * block_len + jnp.arange(block_len, dtype=jnp.int32)
        source = key_offset // stride
        local_key = key_offset % stride
        key_global = (local_key - cache_rows) * shards + source
        present = (key_offset < rows_in)[None, :]
        visible = present & (
            (local_key < cache_rows)[None, :] | (key_global[None, :] <= query_pos[:, None])
        )
        return absorb(state_now, key_block, visible)

    row_max, totals, accumulated = lax.fori_loop(
        0, padded_len // block_len, fold_block, start_state
    )
    attended = (
        (accumulated / totals[:, :, None])
        .reshape(kv_heads, new_dev, group, head_dim)
        .transpose(1, 0, 2, 3)
    )
    attended = attended.reshape(new_dev, 1, heads_here * head_dim).astype(jnp.bfloat16)
    return (attended, fresh.reshape(new_dev, 1, kv_heads, 2 * head_dim))


MESH = pl.DeviceIdType.MESH
XS = 2


def fused_kernel(
    n,
    w_cols,
    vis_hbm,
    target_hbm,
    counts_hbm,
    gain_hbm,
    proj_hbm,
    wq_hbm,
    wkv_hbm,
    cache_hbm,
    cos_hbm,
    sin_hbm,
    attn_ref,
    newkv_ref,
    vis_ref,
    target_ref,
    counts_ref,
    gain_ref,
    proj,
    wq,
    wkv,
    cos_t,
    sin_t,
    cache_all,
    packed,
    incoming,
    pre,
    pre_recv,
    act,
    norm_send,
    norm_all,
    part_kv,
    part_q,
    zsend_kv,
    zrecv_kv,
    zsend_q,
    zrecv_q,
    fresh_all,
    q_rows,
    load_sem,
    s_cache,
    r_cache,
    s_tok,
    r_tok,
    s_pre,
    r_pre,
    s_norm,
    r_norm,
    s_fwd,
    r_fwd,
    s_w,
    r_w,
    s_y,
    r_y,
    s_z,
    r_z,
    s_fresh,
    r_fresh,
):
    s = lax.axis_index("seq")
    m = lax.axis_index("mdl")
    zs = n // XS
    z, x = s // XS, s % XS
    g = lax.axis_index("grp")
    mate = {"mdl": 1 - m}
    beside_x = {"seq": z * XS + 1 - x}
    beside_y = {"grp": 1 - g}
    peers = [(s + k) % n for k in range(n)]

    def send(src, dst, ssem, rsem, device):
        copy = pltpu.make_async_remote_copy(
            src_ref=src,
            dst_ref=dst,
            send_sem=ssem,
            recv_sem=rsem,
            device_id=device,
            device_id_type=MESH,
        )
        copy.start()
        return copy

    barrier = pltpu.get_barrier_semaphore()
    for k in range(1, n):
        pl.semaphore_signal(barrier, inc=1, device_id={"seq": peers[k]}, device_id_type=MESH)
    pl.semaphore_signal(barrier, inc=1, device_id=mate, device_id_type=MESH)
    pl.semaphore_signal(barrier, inc=1, device_id=beside_y, device_id_type=MESH)

    loads = []
    for at, (src, dst) in enumerate(
        (
            (counts_hbm, counts_ref),
            (target_hbm, target_ref),
            (vis_hbm, vis_ref),
            (cache_hbm, cache_all.at[s]),
            (wkv_hbm, wkv.at[x]),
            (wq_hbm, wq.at[x]),
            (proj_hbm, proj),
            (cos_hbm.at[s], cos_t),
            (sin_hbm.at[s], sin_t),
            (gain_hbm, gain_ref),
        )
    ):
        copy = pltpu.make_async_copy(src, dst, load_sem.at[at])
        copy.start()
        loads.append(copy)

    toks = vis_ref.shape[1]
    cap = packed.shape[1]
    slots = n * cap
    new_dev = toks // 2
    loads[0].wait()
    prefix = []
    running = jnp.int32(0)
    here = jnp.int32(0)
    for i in range(n):
        prefix.append(running)
        here = jnp.where(s == i, running, here)
        running = running + counts_ref[i]
    slot = lax.broadcasted_iota(jnp.int32, (slots, toks), 0)
    local_row = ((slot // cap - here) & (n - 1)) + (slot % cap) * n
    loads[1].wait()
    chosen = jnp.where(local_row == target_ref[...], 1.0, 0.0)
    sizes = jnp.sum(chosen, axis=1, keepdims=True)
    loads[2].wait()
    contract = (((1,), (1,)), ((), ()))
    summed = lax.dot_general(
        chosen.astype(jnp.bfloat16), vis_ref[...], contract, preferred_element_type=jnp.float32
    )
    merged = (summed / jnp.where(sizes > 0.0, sizes, 1.0)).astype(jnp.bfloat16)
    packed[...] = merged.reshape(packed.shape)

    pl.semaphore_wait(barrier, n + 1)
    tok_copies = [
        send(packed.at[peers[k]], incoming.at[s], s_tok.at[k], r_tok.at[k], {"seq": peers[k]})
        for k in range(1, n)
    ]
    depth = wq.shape[1]
    loads[4].wait()
    loads[5].wait()
    pieces = []
    at = pl.ds(pl.multiple_of(g * (depth // 2), 16), depth // 2)
    pieces.append((wkv.at[x, at], wkv.at[1 - x, at]))
    for cols in w_cols:
        pieces.append((wq.at[x, at, pl.ds(*cols)], wq.at[1 - x, at, pl.ds(*cols)]))
    straight = [
        send(src, src, s_w.at[at], r_w.at[at], beside_x) for at, (src, _) in enumerate(pieces)
    ]

    def pass_on(which):
        copies = []
        for at in which:
            straight[at].wait()
            dst = pieces[at][1]
            copies.append(send(dst, dst, s_y.at[at], r_y.at[at], beside_y))
        return copies

    loads[3].wait()
    cache_copies = [
        send(
            cache_all.at[s],
            cache_all.at[s],
            s_cache.at[k],
            r_cache.at[k],
            {"seq": (z + k) % zs * XS + x},
        )
        for k in range(1, zs)
    ]

    def share_x(buffer, copies, ssem, rsem):
        shared = [send(buffer.at[s], buffer.at[s], ssem.at[zs], rsem.at[zs], beside_x)]
        for k in range(1, zs):
            copies[k - 1].wait()
            came = buffer.at[(z + zs - k) % zs * XS + x]
            shared.append(send(came, came, ssem.at[zs + k], rsem.at[zs + k], beside_x))
        return shared

    incoming[s] = packed[s]

    column = lax.broadcasted_iota(jnp.int32, (new_dev, slots), 1)
    source = column // cap
    starts = jnp.zeros_like(column)
    ends = jnp.zeros_like(column)
    for i in range(n):
        starts = jnp.where(source == i, prefix[i], starts)
        ends = jnp.where(source == i, prefix[i] + counts_ref[i], ends)
    global_row = starts + ((s - starts) & (n - 1)) + (column % cap) * n
    goal = jnp.where(global_row < ends, global_row // n, -1)
    placing = jnp.where(
        goal == lax.broadcasted_iota(jnp.int32, (new_dev, slots), 0), 1.0, 0.0
    ).astype(jnp.bfloat16)
    loads[6].wait()
    for copy in tok_copies:
        copy.wait()
    rows = jnp.dot(
        placing,
        incoming[...].reshape(slots, incoming.shape[2]),
        preferred_element_type=jnp.float32,
    ).astype(jnp.bfloat16)

    width = proj.shape[1]
    half = new_dev // 2
    step = 512
    mine = pl.ds(pl.multiple_of(m * half, half), half)
    other = pl.ds(pl.multiple_of((1 - m) * half, half), half)
    pre_copies = []
    for c in range(width // step):
        cols = pl.ds(c * step, step)
        pre[c] = jnp.dot(rows, proj[:, cols], preferred_element_type=jnp.float32)
        pre_copies.append(
            send(pre.at[c, other], pre_recv.at[c], s_pre.at[c], r_pre.at[c], mate)
        )
    square = jnp.zeros((half, step), jnp.float32)
    for c in range(width // step):
        pre_copies[c].wait()
        value = pre[c, mine] + pre_recv[c]
        value = 0.5 * value * (1.0 + lax.erf(value * (1.0 / math.sqrt(2.0))))
        square = square + value * value
        act[:, pl.ds(c * step, step)] = value
    mean = jnp.sum(square, axis=1, keepdims=True) / width
    inv_rms = lax.rsqrt(mean + norm_eps)
    loads[9].wait()
    lane = gain_ref.shape[1]
    normed = jnp.concatenate(
        [
            (act[:, pl.ds(j * lane, lane)] * inv_rms * gain_ref[pl.ds(j, 1), :]).astype(
                jnp.bfloat16
            )
            for j in range(width // lane)
        ],
        axis=1,
    )
    wide = width // zs
    for d in range(zs):
        norm_send[d] = normed[:, d * wide : (d + 1) * wide]
    norm_copies = []
    for k in range(1, zs):
        zt = (z + k) % zs
        norm_copies.append(
            send(
                norm_send.at[zt],
                norm_all.at[z, m],
                s_norm.at[k],
                r_norm.at[k],
                {"seq": zt * XS + x},
            )
        )
    norm_all[z, m] = norm_send[z]
    forwards = [send(norm_all.at[z, m], norm_all.at[z, m], s_fwd.at[0], r_fwd.at[0], mate)]
    early = 1 + len(pieces) // 2
    crossing = pass_on(range(early))
    for k in range(1, zs):
        norm_copies[k - 1].wait()
        came = norm_all.at[(z + zs - k) % zs, m]
        forwards.append(send(came, came, s_fwd.at[k], r_fwd.at[k], mate))
    crossing = crossing + pass_on(range(early, len(pieces)))
    for copy in forwards:
        copy.wait()
    crossing[0].wait()

    lhs = norm_all[...].reshape(zs * new_dev, wide)
    order = [(z + k) % zs for k in range(1, zs)]

    def along_z(which, weight, part, zsend, zrecv):
        part[...] = jnp.dot(
            lhs, weight[...].reshape(wide, weight.shape[2]), preferred_element_type=jnp.float32
        ).reshape(part.shape)
        copies = []
        for k, zt in enumerate(order):
            zsend[k] = part[zt].astype(jnp.bfloat16)
            copies.append(
                send(
                    zsend.at[k],
                    zrecv.at[k],
                    s_z.at[which, k],
                    r_z.at[which, k],
                    {"seq": zt * XS + x},
                )
            )
        return part[z], copies

    def finish(total, copies, zrecv):
        for k, copy in enumerate(copies):
            copy.wait()
            total = total + zrecv[k].astype(jnp.float32)
        return total

    head = cos_t.shape[1]
    kv_own, kv_copies = along_z(0, wkv, part_kv, zsend_kv, zrecv_kv)
    cache_shared = share_x(cache_all, cache_copies, s_cache, r_cache)
    loads[7].wait()
    loads[8].wait()
    cosine, sine = cos_t[...], sin_t[...]

    def turn(value):
        return value * cosine + pltpu.roll(value, head // 2, 1) * sine

    total = finish(kv_own, kv_copies, zrecv_kv)
    fresh = jnp.concatenate([turn(total[:, :head]), total[:, head:]], axis=1).astype(jnp.bfloat16)
    fresh_all[s] = fresh
    newkv_ref[...] = fresh
    fresh_copies = [
        send(
            fresh_all.at[s],
            fresh_all.at[s],
            s_fresh.at[k],
            r_fresh.at[k],
            {"seq": (z + k) % zs * XS + x},
        )
        for k in range(1, zs)
    ]
    q_sums = []
    for c, cols in enumerate(w_cols):
        crossing[1 + c].wait()
        q_sums.append(
            along_z(1 + c, *(ref.at[:, :, pl.ds(*cols)] for ref in (wq, part_q, zsend_q, zrecv_q)))
        )
    fresh_shared = share_x(fresh_all, fresh_copies, s_fresh, r_fresh)
    total = jnp.concatenate(
        [
            finish(own, copies, zrecv_q.at[:, :, pl.ds(*cols)])
            for (own, copies), cols in zip(q_sums, w_cols)
        ],
        axis=1,
    )
    heads = total.shape[1] // head
    for h in range(heads):
        q_rows[pl.ds(h * new_dev, new_dev), :] = turn(
            total[:, h * head : (h + 1) * head]
        ).astype(jnp.bfloat16)
    for copy in cache_shared:
        copy.wait()
    for copy in fresh_shared:
        copy.wait()

    kept = cache_all.shape[0] * cache_all.shape[1]
    old = cache_all[...].reshape(kept, 2 * head)
    new = fresh_all[...].reshape(n * new_dev, 2 * head)
    queries = q_rows[...]
    scale = 1.0 / math.sqrt(head)
    old_score = (
        lax.dot_general(queries, old[:, :head], contract, preferred_element_type=jnp.float32) * scale
    )
    new_score = (
        lax.dot_general(queries, new[:, :head], contract, preferred_element_type=jnp.float32) * scale
    )
    lanes = heads * new_dev
    key_at = lax.broadcasted_iota(jnp.int32, (lanes, n * new_dev), 1)
    query_at = lax.broadcasted_iota(jnp.int32, (lanes, n * new_dev), 0)
    visible = (key_at % new_dev) * n + key_at // new_dev <= (query_at % new_dev) * n + s
    new_score = jnp.where(visible, new_score, mask_fill)
    top = jnp.maximum(
        jnp.max(old_score, axis=1, keepdims=True), jnp.max(new_score, axis=1, keepdims=True)
    )
    old_weight = jnp.exp(old_score - top)
    new_weight = jnp.where(visible, jnp.exp(new_score - top), 0.0)
    totals = jnp.sum(old_weight, axis=1, keepdims=True) + jnp.sum(new_weight, axis=1, keepdims=True)
    mixed = jnp.dot(
        old_weight.astype(jnp.bfloat16), old[:, head:], preferred_element_type=jnp.float32
    ) + jnp.dot(new_weight.astype(jnp.bfloat16), new[:, head:], preferred_element_type=jnp.float32)
    attended = (mixed / totals).astype(jnp.bfloat16)
    for h in range(heads):
        attn_ref[:, pl.ds(h * head, head)] = attended[h * new_dev : (h + 1) * new_dev]


def fused_plan(
    vis_tokens,
    merge_target,
    merged_counts,
    proj_weight,
    norm_gain,
    query_weight,
    keyval_weight,
    cache_kv,
):
    n = lax.axis_size("seq")
    zs = n // XS
    toks, feat = vis_tokens.shape
    new_dev = toks // 2
    half = new_dev // 2
    cap = (new_dev + 3 * (new_dev // 3) + n - 1) // n
    width = proj_weight.shape[1]
    depth, qcols = query_weight.shape
    kvcols = keyval_weight.shape[2]
    head = kvcols // 2
    cached = cache_kv.shape[0]
    pos = (
        cached * n + np.arange(new_dev, dtype=np.float32)[None, :] * n
        + np.arange(n, dtype=np.float32)[:, None]
    ).astype(np.float32)
    freq = np.power(
        np.float32(theta_base), np.float32(-2.0) * np.arange(head // 2, dtype=np.float32) / np.float32(head)
    ).astype(np.float32)
    angles = (pos[:, :, None] * freq[None, None, :]).astype(np.float64)
    cos_table = np.concatenate([np.cos(angles)] * 2, axis=-1).astype(np.float32)
    sin_table = np.concatenate([-np.sin(angles), np.sin(angles)], axis=-1).astype(np.float32)
    bf, f32 = jnp.bfloat16, jnp.float32
    chunks = width // 512
    w_cols = [(at, min(256, qcols - at)) for at in range(0, qcols, 256)]
    pieces = 1 + len(w_cols)
    vm, dma = pltpu.VMEM, pltpu.SemaphoreType.DMA
    scratch = [
        vm((feat, toks), bf),
        vm((1, toks), jnp.int32),
        pltpu.SMEM((n,), jnp.int32),
        vm((width // 128, 128), f32),
        vm((feat, width), bf),
        vm((XS, depth, qcols), bf),
        vm((XS, depth, kvcols), bf),
        vm((new_dev, head), f32),
        vm((new_dev, head), f32),
        vm((n, cached, kvcols), bf),
        vm((n, cap, feat), bf),
        vm((n, cap, feat), bf),
        vm((chunks, new_dev, 512), f32),
        vm((chunks, half, 512), f32),
        vm((half, width), f32),
        vm((zs, half, depth * XS), bf),
        vm((zs, 2, half, depth * XS), bf),
        vm((zs, new_dev, kvcols), f32),
        vm((zs, new_dev, qcols), f32),
        vm((zs - 1, new_dev, kvcols), bf),
        vm((zs - 1, new_dev, kvcols), bf),
        vm((zs - 1, new_dev, qcols), bf),
        vm((zs - 1, new_dev, qcols), bf),
        vm((n, new_dev, kvcols), bf),
        vm((qcols // head * new_dev, head), bf),
        dma((10,)),
        dma((n,)),
        dma((n,)),
        dma((n,)),
        dma((n,)),
        dma((chunks,)),
        dma((chunks,)),
        dma((n,)),
        dma((n,)),
        dma((n,)),
        dma((n,)),
        dma((pieces,)),
        dma((pieces,)),
        dma((pieces,)),
        dma((pieces,)),
        dma((pieces, zs)),
        dma((pieces, zs)),
        dma((n,)),
        dma((n,)),
    ]
    in_vmem = pl.BlockSpec(memory_space=pltpu.VMEM)
    in_hbm = pl.BlockSpec(memory_space=pltpu.HBM)
    attended, fresh = pl.pallas_call(
        functools.partial(fused_kernel, n, w_cols),
        out_shape=(
            pltpu.VMEM((new_dev, qcols), bf),
            pltpu.VMEM((new_dev, kvcols), bf),
        ),
        in_specs=[in_hbm] * 10,
        out_specs=(in_vmem, in_vmem),
        scratch_shapes=scratch,
        compiler_params=pltpu.CompilerParams(
            collective_id=0, has_side_effects=True, vmem_limit_bytes=60 * 1024 * 1024
        ),
    )(
        vis_tokens.T,
        merge_target.reshape(1, toks),
        merged_counts,
        norm_gain.reshape(width // 128, 128),
        proj_weight,
        query_weight,
        keyval_weight.reshape(depth, kvcols),
        cache_kv.reshape(cached, kvcols),
        jnp.asarray(cos_table),
        jnp.asarray(sin_table),
    )
    return (
        attended.reshape(new_dev, 1, qcols),
        fresh.reshape(new_dev, 1, keyval_weight.shape[1], kvcols),
    )


def solution(mesh):
    placed = (
        P(("grp", "seq"), "mdl"),
        P(("grp", "seq")),
        P("grp"),
        P("mdl", None),
        P(),
        P("seq", "mdl"),
        P("seq", "mdl", None),
        P(("grp", "seq"), "mdl", None),
    )
    small = mesh.shape["seq"] == 8 and mesh.shape["grp"] == 2
    per_device = fused_plan if small else plain_plan
    return jax.shard_map(
        per_device,
        mesh=mesh,
        in_specs=placed,
        out_specs=(P(None, ("grp", "seq"), "mdl"), P(None, ("grp", "seq"), "mdl", None)),
        check_vma=False,
    )
```
